128 devices in a mesh: region: 4 (over z_hi, core), dev: 32 (over x, y, z_lo).
Axes of the slice: x: 4, y: 4, z: 4 (z_hi: 2, z_lo: 2; z = z_hi * 2 + z_lo), core: 2. Of those that a mesh axis runs over, the one named last changes fastest.
Arguments:
- science: float32 [4, 32, 2, 1024, 2, 128], P('region', 'dev'), may hold values from -6 to 6, as said below
- coadd: float32 [4, 4096, 2, 128], P('region', 'dev'), may hold values from -6 to 6, as said below
- coefficients: float32 [4, 32, 2, 31, 3], P('region', 'dev'), may hold values from -1 to 1
- strip_start: int32 [4, 32, 2], P('region', 'dev'), may hold values from 0 to 24, as said below
Outputs:
- patch_sums: float32 [4, 4096, 2, 128], P('region', 'dev')
The draws below stay inside these ranges and needn't reach their ends.
Inputs may be any that keep to these rules, and one draw needn't show every extreme that they name: Strip e of a device covers blocks strip_start .. strip_start + 7 of its region; the two strips of one device cover 2 * 8 different blocks; no block is covered by more than 32 strips, and in every region some block is covered by a strip of every device of the region; some region has a strip starting at 0 and some region one starting at 24. `science`: plane 1 holds positive variances. `coadd`: plane 1 holds positive variances.
All inputs are finite; a program needn't handle non-finite values.
Results may differ from the reference program's by a relative error of at most 0.0001.
Values sent between devices are 32-bit elements; how exact they have to be, the bound alone decides.
A program may use at most 64 MiB of HBM per device.

```python
import math
import jax
import jax.numpy as jnp
from jax import lax

BLK = 128
CW = 128
EXP_DEV = 2
KSIZE = 21
NPROF = 12
NBASIS = 31
NPOLY = 3
STRIP = 8
N_REGION = 4
N_DEV = 32


def draw_science(key, part):
    flux_key, noise_key = jax.random.split(key, 2)
    shape = (N_REGION, N_DEV, EXP_DEV, STRIP * BLK, CW)
    flux_plane = jnp.clip(jax.random.normal(flux_key, shape, jnp.float32), -6.0, 6.0)
    variance_plane = jnp.exp(jax.random.uniform(noise_key, shape, jnp.float32, math.log(0.5), math.log(4.0)))
    return jnp.stack([flux_plane, variance_plane], axis=4)


def draw_coadd(key, part):
    flux_key, noise_key = jax.random.split(key, 2)
    shape = (N_REGION, N_DEV * BLK, CW)
    flux_plane = jnp.clip(jax.random.normal(flux_key, shape, jnp.float32), -6.0, 6.0)
    variance_plane = jnp.exp(jax.random.uniform(noise_key, shape, jnp.float32, math.log(0.1), math.log(1.0)))
    return jnp.stack([flux_plane, variance_plane], axis=2)


def draw_strip_start(key, part):
    quarter = N_DEV // 4
    flip_key, rest_key = jax.random.split(jax.random.fold_in(key, 17), 2)
    flip_bit = jax.random.randint(flip_key, (), 0, 2).astype(jnp.int32)
    region_keys = jax.random.split(rest_key, N_REGION)
    collected = []
    for region_number in range(N_REGION):
        shuffled = jax.random.permutation(region_keys[region_number], N_DEV)
        placing = jnp.argsort(shuffled).astype(jnp.int32)
        lower_start = placing // 4
        drawn = jnp.stack([lower_start, lower_start + 2 * quarter], axis=1)
        mirrored = N_DEV - quarter - drawn
        mirror_flag = (region_number + flip_bit) % 2
        collected.append(jnp.where(mirror_flag == 1, mirrored, drawn))
    return jnp.stack(collected).astype(jnp.int32)


def block_levels(own_key, shape, shards, smallest, top_value):
    level = 1.0
    for axis_at, shards_of in shards:
        steps = jax.random.uniform(jax.random.fold_in(jax.random.fold_in(own_key, 6), axis_at), (shards_of,), jnp.float32, smallest / len(shards), top_value / len(shards))
        level = level * jnp.repeat(jnp.exp(steps), shape[axis_at] // shards_of).reshape((-1,) + (1,) * (len(shape) - 1 - axis_at))
    return level


def bell_draw(stream_key, extent, scale, limit, shards=(), held_as=jnp.bfloat16):
    array = scale * jax.random.normal(stream_key, extent, jnp.float32)
    if shards:
        array = array * block_levels(stream_key, extent, shards, -0.22, 0.18)
    return jnp.clip(array, -limit, limit).astype(held_as)


def setup_inputs(seed: int = 0) -> dict:
    splits = jax.random.split(jax.random.key(seed), 5)
    return {
        "science": draw_science(jax.random.fold_in(splits[4], 71), 0),
        "coadd": draw_coadd(jax.random.fold_in(splits[4], 71), 0),
        "coefficients": bell_draw(splits[2], (N_REGION, N_DEV, EXP_DEV, NBASIS, NPOLY), 0.2, 1.0, ((0, 4), (1, 32)), jnp.float32),
        "strip_start": draw_strip_start(jax.random.fold_in(splits[4], 71), 0),
    }


SPREADS = (1.0, 2.0, 4.0)
DEGREES = (4, 3, 2)


def profile_values(offset, spread, exponent):
    half_width = (KSIZE - 1) // 2
    scaled = offset / half_width
    return scaled ** exponent * jnp.exp(-offset * offset / (2.0 * spread * spread))


def profile_list():
    entries = []
    for spread, degree in zip(SPREADS, DEGREES):
        for exponent in range(degree + 1):
            entries.append((spread, exponent))
    return entries


def profile_grid():
    taps = jnp.arange(KSIZE, dtype=jnp.float32) - (KSIZE - 1) // 2
    collected = []
    for spread, exponent in profile_list():
        values = profile_values(taps, spread, exponent)
        collected.append(values / jnp.sum(jnp.abs(values)))
    return jnp.stack(collected)


def basis_list():
    listing = []
    offset = 0
    for degree in DEGREES:
        for vertical in range(degree + 1):
            for across in range(degree + 1 - vertical):
                listing.append((offset + vertical, offset + across))
        offset = offset + degree + 1
    return listing


def strip_terms(window, strip_data, spatial_terms, grid, listing):
    half_width = (KSIZE - 1) // 2
    strip_rows = STRIP * BLK
    flux_plane = window[:, 0, :]
    padded_cols = jnp.pad(flux_plane, ((0, 0), (half_width, half_width)))
    horizontal = []
    for profile in range(NPROF):
        running = jnp.zeros_like(flux_plane)
        for tap_index in range(KSIZE):
            running = running + grid[profile, tap_index] * padded_cols[:, tap_index:tap_index + CW]
        horizontal.append(running)
    column_coords = (2.0 * jnp.arange(CW, dtype=jnp.float32) + 1.0) / CW - 1.0
    row_coords = (2.0 * jnp.arange(strip_rows, dtype=jnp.float32) + 1.0) / strip_rows - 1.0
    profile_sums = jnp.sum(grid, axis=1)
    model_image = jnp.zeros((strip_rows, CW), jnp.float32)
    kernel_sum = jnp.zeros((strip_rows, CW), jnp.float32)
    for number, (vertical, across) in enumerate(listing):
        smooth = jnp.zeros((strip_rows, CW), jnp.float32)
        for tap_index in range(KSIZE):
            smooth = smooth + grid[vertical, tap_index] * horizontal[across][tap_index:tap_index + strip_rows]
        factor = (spatial_terms[number, 0] + spatial_terms[number, 1] * column_coords[None, :]
                  + spatial_terms[number, 2] * row_coords[:, None])
        model_image = model_image + factor * smooth
        kernel_sum = kernel_sum + factor * (profile_sums[vertical] * profile_sums[across])
    variance = strip_data[:, 1, :] + kernel_sum * kernel_sum * window[half_width:half_width + strip_rows, 1, :]
    weight = 1.0 / variance
    return jnp.stack([(strip_data[:, 0, :] - model_image) * weight, weight], axis=1)


def reference(science, coadd, coefficients, strip_start):
    half_width = (KSIZE - 1) // 2
    region_rows = N_DEV * BLK
    strip_rows = STRIP * BLK
    grid = profile_grid()
    listing = basis_list()
    sky_rows = coadd.reshape(N_REGION * region_rows, 2, CW)
    padded = jnp.pad(sky_rows, ((half_width, half_width), (0, 0), (0, 0)))
    strip_items = science.reshape(-1, strip_rows, 2, CW)
    spatial_all = coefficients.reshape(-1, NBASIS, NPOLY)
    start_blocks = strip_start.reshape(-1).astype(jnp.int32)
    region_ids = (jnp.arange(start_blocks.shape[0], dtype=jnp.int32) // (N_DEV * EXP_DEV)).astype(jnp.int32)
    first_rows = (region_ids * region_rows + start_blocks * BLK).astype(jnp.int32)

    def accumulate(running, element):
        strip_data, spatial_terms, first_row = element
        window = lax.dynamic_slice_in_dim(padded, first_row, strip_rows + 2 * half_width, 0)
        contributions = strip_terms(window, strip_data, spatial_terms, grid, listing)
        current = lax.dynamic_slice_in_dim(running, first_row, strip_rows, 0)
        return lax.dynamic_update_slice_in_dim(running, current + contributions, first_row, 0), None

    running, unused = lax.scan(accumulate, jnp.zeros(sky_rows.shape, jnp.float32),
                               (strip_items, spatial_all, first_rows))
    return running.reshape(N_REGION, region_rows, 2, CW)
```

```python
import jax
import jax.numpy as jnp
import ml_dtypes
import numpy as np
from jax import lax
from jax.experimental import pallas as pl
from jax.experimental.pallas import tpu as pltpu
from jax.sharding import PartitionSpec as P

BLK = 128
CW = 128
KSIZE = 21
NPROF = 12
NBASIS = 31
SPREADS = (1.0, 2.0, 4.0)
DEGREES = (4, 3, 2)

RES = 8
NX = 4
EDGE = 16
EXT = BLK + 2 * EDGE
DEPTH = 512
HALF = BLK // 2
F32 = jnp.float32
BF16 = jnp.bfloat16
MESH = pl.DeviceIdType.MESH


def basis_list():
    listing = []
    offset = 0
    for degree in DEGREES:
        for vertical in range(degree + 1):
            for across in range(degree + 1 - vertical):
                listing.append((offset + vertical, offset + across))
        offset = offset + degree + 1
    return listing


BASIS = basis_list()


def profiles():
    half_width = (KSIZE - 1) // 2
    taps = np.arange(KSIZE, dtype=np.float64) - half_width
    rows = []
    for spread, degree in zip(SPREADS, DEGREES):
        for exponent in range(degree + 1):
            values = (taps / half_width) ** exponent * np.exp(-taps * taps / (2.0 * spread * spread))
            rows.append(values / np.abs(values).sum())
    return np.stack(rows)


def split_np(matrix):
    high = matrix.astype(np.float32).astype(ml_dtypes.bfloat16)
    low = (matrix - high.astype(np.float64)).astype(np.float32).astype(ml_dtypes.bfloat16)
    return high, low


def constant_matrices():
    half_width = (KSIZE - 1) // 2
    prof = profiles()
    wide = np.zeros((CW, NPROF, CW))
    for target in range(CW):
        for tap in range(KSIZE):
            source = target + tap - half_width
            if 0 <= source < CW:
                wide[source, :, target] = prof[:, tap]
    high, low = split_np(wide.reshape(CW, NPROF // 2, 2 * CW).transpose(1, 0, 2))
    across = np.concatenate([high, high, low], axis=1)
    tall = np.zeros((NPROF, BLK, EXT))
    for target in range(BLK):
        for tap in range(KSIZE):
            tall[:, target, EDGE + target + tap - half_width] = prof[:, tap]
    high, low = split_np(tall)
    pad = np.zeros((NPROF, BLK, DEPTH - 3 * EXT), ml_dtypes.bfloat16)
    down = np.concatenate([high, low, high, pad], axis=2).reshape(NPROF * BLK, DEPTH)
    sums = prof.sum(axis=1)
    norms = np.zeros((1, CW), np.float32)
    for number, (vertical, horizontal) in enumerate(BASIS):
        norms[0, number] = sums[vertical] * sums[horizontal]
    return across, down, norms


def kernel(
    regions,
    sci_hbm, sky_hbm, coef_ref, start_ref, across_hbm, down_hbm, norm_ref,
    out_ref,
    sci, pack, recv, sky, edge, across, down, wide, basis, skyvar,
    acc, part, tab, tabs, num, nums, tab_s, num_s,
    loc_sem, sky_ss, sky_rs, edge_ss, edge_rs, fwd_ss, fwd_rs,
    tab_ss, tab_rs, num_ss, num_rs, sci_ss, sci_rs, red_ss, red_rs,
):
    region = lax.axis_index("region")
    dev = lax.axis_index("dev")
    x = dev // RES
    r = dev % RES
    y = r // 2
    z = r % 2
    total_devs = regions * RES * NX
    whole = region * (RES * NX) + dev

    def peer(t):
        return ((y + t // 2) % 4) * 2 + (z + t % 2) % 2

    def giver(t):
        return ((y + 4 - t // 2) % 4) * 2 + (z + t % 2) % 2

    def plane_id(res):
        return {"dev": x * RES + res}

    def line_id(dx):
        return {"dev": ((x + dx) % NX) * RES + r}

    def sky_id(step):
        other = (whole + step + total_devs) % total_devs
        return {"region": other // (RES * NX), "dev": other % (RES * NX)}

    def sci_copy(h, t, slot):
        return pltpu.make_async_remote_copy(
            src_ref=pack.at[h, t], dst_ref=recv.at[h, slot],
            send_sem=sci_ss.at[h, t], recv_sem=sci_rs.at[h, slot],
            device_id=plane_id(peer(t)), device_id_type=MESH)

    def tab_copy(t, slot):
        return pltpu.make_async_remote_copy(
            src_ref=tab, dst_ref=tabs.at[slot],
            send_sem=tab_ss.at[t], recv_sem=tab_rs.at[slot],
            device_id=plane_id(peer(t)), device_id_type=MESH)

    def num_copy(t, slot):
        return pltpu.make_async_remote_copy(
            src_ref=num, dst_ref=nums.at[slot],
            send_sem=num_ss.at[t], recv_sem=num_rs.at[slot],
            device_id=plane_id(peer(t)), device_id_type=MESH)

    def sky_copy(dx, slot):
        return pltpu.make_async_remote_copy(
            src_ref=sky.at[x], dst_ref=sky.at[slot],
            send_sem=sky_ss.at[dx], recv_sem=sky_rs.at[slot],
            device_id=line_id(dx), device_id_type=MESH)

    def fwd_copy(dx, slot):
        return pltpu.make_async_remote_copy(
            src_ref=edge.at[x], dst_ref=edge.at[slot],
            send_sem=fwd_ss.at[dx], recv_sem=fwd_rs.at[slot],
            device_id=line_id(dx), device_id_type=MESH)

    def edge_copy(side):
        rows = pl.ds(2 * (BLK - EDGE), 2 * EDGE) if side == 0 else pl.ds(0, 2 * EDGE)
        return pltpu.make_async_remote_copy(
            src_ref=sky.at[x, rows], dst_ref=edge.at[x_of(side), side],
            send_sem=edge_ss.at[side], recv_sem=edge_rs.at[side],
            device_id=sky_id(1 if side == 0 else -1), device_id_type=MESH)

    def x_of(side):
        other = (whole + (1 if side == 0 else -1) + total_devs) % total_devs
        return (other % (RES * NX)) // RES

    def edge_arrival(side):
        rows = pl.ds(2 * (BLK - EDGE), 2 * EDGE) if side == 0 else pl.ds(0, 2 * EDGE)
        return pltpu.make_async_remote_copy(
            src_ref=sky.at[x, rows], dst_ref=edge.at[x, side],
            send_sem=edge_ss.at[side], recv_sem=edge_rs.at[side],
            device_id=sky_id(1 if side == 0 else -1), device_id_type=MESH)

    def red_copy(h, dx, slot):
        return pltpu.make_async_remote_copy(
            src_ref=acc.at[h, (x + dx) % NX], dst_ref=part.at[h, slot],
            send_sem=red_ss.at[h, dx], recv_sem=red_rs.at[h, slot],
            device_id=line_id(dx), device_id_type=MESH)

    sky_load = pltpu.make_async_copy(sky_hbm, sky.at[x], loc_sem.at[0])
    sky_load.start()
    sci_load = pltpu.make_async_copy(sci_hbm, sci, loc_sem.at[1])
    sci_load.start()
    across_load = pltpu.make_async_copy(across_hbm, across, loc_sem.at[2])
    across_load.start()
    down_load = pltpu.make_async_copy(down_hbm, down, loc_sem.at[3])
    down_load.start()

    barrier = pltpu.get_barrier_semaphore()

    def greet(t, carry):
        pl.semaphore_signal(barrier, inc=1, device_id=plane_id(peer(t)), device_id_type=MESH)
        return carry

    lax.fori_loop(1, RES, greet, 0)
    for dx in range(1, NX):
        pl.semaphore_signal(barrier, inc=1, device_id=line_id(dx), device_id_type=MESH)
    for step in (1, -1):
        pl.semaphore_signal(barrier, inc=1, device_id=sky_id(step), device_id_type=MESH)

    lanes = lax.broadcasted_iota(jnp.int32, (8, CW), 1)
    sublanes = lax.broadcasted_iota(jnp.int32, (8, CW), 0)
    tab[...] = jnp.zeros((8, CW), F32)
    for term in range(3):
        tab[2 * term : 2 * term + 2, 0:NBASIS] = coef_ref[term]
    raw = tab[...]
    weighted = jnp.sum(raw * norm_ref[...], axis=1, keepdims=True)
    tab[...] = jnp.where(lanes == NBASIS, weighted, raw)
    start0 = start_ref[0, 0]
    start1 = start_ref[0, 1]
    num[...] = jnp.where(lanes == 0, start0, start1) + 0 * sublanes
    tabs[r] = tab[...]
    nums[r] = num[...]

    sky_load.wait()
    pl.semaphore_wait(barrier, RES - 1 + NX - 1 + 2)

    for side in (0, 1):
        edge_copy(side).start()
    for dx in range(1, NX):
        sky_copy(dx, x).start()
    sci_load.wait()

    starts = (start0, start1)

    def chosen(h, res, e):
        block = lax.rem(res - starts[e] + 4 * RES, RES)
        return sci[e, block, h]

    for h in range(2):
        for e in range(2):
            recv[h, r, e] = chosen(h, r, e)

        def give(t, carry):
            for e in range(2):
                pack[h, t, e] = chosen(h, peer(t), e)
            sci_copy(h, t, r).start()
            if h == 0:
                tab_copy(t, r).start()
                num_copy(t, r).start()
            return carry

        lax.fori_loop(1, RES, give, 0)

    for side in (0, 1):
        edge_arrival(side).wait_recv()
    for dx in range(1, NX):
        fwd_copy(dx, x).start()

    acc[...] = jnp.zeros(acc.shape, F32)
    across_load.wait()
    down_load.wait()

    first = (whole == 0) | ((region == 0) & (r == 0))
    last = (region == regions - 1) & (r == RES - 1)

    def spread_across(block):
        top = edge[block, 0, pl.ds(0, EDGE, stride=2), :]
        low = edge[block, 1, pl.ds(0, EDGE, stride=2), :]
        top = jnp.where(first & (block == 0), 0.0, top)
        low = jnp.where(last & (block == NX - 1), 0.0, low)
        body = sky[block, pl.ds(0, BLK, stride=2), :]
        for h in range(2):
            skyvar[block, h] = sky[block, pl.ds(h * BLK + 1, HALF, stride=2), :]
        full = jnp.concatenate([top, body, low], axis=0)
        high = full.astype(BF16)
        rest = (full - high.astype(F32)).astype(BF16)
        lhs = jnp.concatenate([high, rest, high], axis=1)
        return lhs

    for block in range(NX):
        @pl.when(block != x)
        def _():
            sky_copy(1, block).wait_recv()
            fwd_copy(1, block).wait_recv()

        lhs = spread_across(block)
        pair, side = block // 2, block % 2
        columns = slice(side * CW, (side + 1) * CW)

        def tile(q, carry):
            both = jnp.dot(lhs, across[q], preferred_element_type=F32)
            for half in range(2):
                values = both[:, half * CW : (half + 1) * CW]
                high = values.astype(BF16)
                rest = (values - high.astype(F32)).astype(BF16)
                profile = 2 * q + half
                wide[pair, profile, 0:EXT, columns] = high
                wide[pair, profile, EXT : 2 * EXT, columns] = high
                wide[pair, profile, 2 * EXT : 3 * EXT, columns] = rest
            return carry

        lax.fori_loop(0, NPROF // 2, tile, 0)

    for pair in range(2):
        for profile in range(NPROF):
            wide[pair, profile, 3 * EXT : DEPTH, :] = jnp.zeros((DEPTH - 3 * EXT, 2 * CW), BF16)

    def smooth(pair, carry):
        for across_profile in range(NPROF):
            users = [(k, v) for k, (v, a) in enumerate(BASIS) if a == across_profile]
            low_v = users[0][1]
            result = jnp.dot(
                down[low_v * BLK : (low_v + len(users)) * BLK, :],
                wide[pair, across_profile],
                preferred_element_type=F32)
            for place, (k, v) in enumerate(users):
                for side in range(2):
                    for h in range(2):
                        row = place * BLK + h * HALF
                        basis[2 * pair + side, k, h] = result[row : row + HALF, side * CW : (side + 1) * CW]
        return carry

    lax.fori_loop(0, 2, smooth, 0)

    def tables(t, carry):
        tab_copy(t, giver(t)).wait_recv()
        num_copy(t, giver(t)).wait_recv()
        return carry

    lax.fori_loop(1, RES, tables, 0)
    tab_move = pltpu.make_async_copy(tabs, tab_s, loc_sem.at[4])
    tab_move.start()
    num_move = pltpu.make_async_copy(nums, num_s, loc_sem.at[5])
    num_move.start()
    tab_move.wait()
    num_move.wait()

    xs = (2.0 * lanes.astype(F32) + 1.0) / CW - 1.0
    rows = (8 * lax.broadcasted_iota(jnp.int32, (8, 8, CW), 0)
            + lax.broadcasted_iota(jnp.int32, (8, 8, CW), 1)).astype(F32)
    ys_base = (2.0 * rows + 1.0) / (RES * BLK)

    def work(h, t):
        source = giver(t)
        found = []
        for e in range(2):
            start = num_s[source, 0, e]
            place = lax.rem(r - start + 4 * RES, RES)
            block = (start + place) // RES
            flat = jnp.zeros((8, 8, CW), F32)
            slope = jnp.zeros((8, 8, CW), F32)
            for k in range(NBASIS):
                image = basis[block, k, h].reshape(8, 8, CW)
                factor = tab_s[source, e, k] + tab_s[source, 2 + e, k] * xs
                flat = flat + factor[None] * image
                slope = slope + tab_s[source, 4 + e, k] * image
            y0 = (place * BLK + h * HALF).astype(F32)
            ys = ys_base + (y0 * (2.0 / (RES * BLK)) - 1.0)
            gain = (tab_s[source, e, NBASIS] + tab_s[source, 2 + e, NBASIS] * xs)[None] + tab_s[
                source, 4 + e, NBASIS] * ys
            flux = recv[h, source, e, pl.ds(0, HALF, stride=2), :].reshape(8, 8, CW)
            noise = recv[h, source, e, pl.ds(1, HALF, stride=2), :].reshape(8, 8, CW)
            behind = skyvar[block, h].reshape(8, 8, CW)
            weight = 1.0 / (noise + gain * gain * behind)
            diff = (flux - (flat + ys * slope)) * weight
            found.append((block, diff.reshape(HALF, CW), weight.reshape(HALF, CW)))
        for target in range(NX):
            for plane in range(2):
                span = slice(plane * HALF, (plane + 1) * HALF)
                old = acc[h, target, span, :]
                for block, diff, weight in found:
                    old = old + jnp.where(block == target, weight if plane else diff, 0.0)
                acc[h, target, span, :] = old

    for h in range(2):
        work(h, 0)

        def take(t, carry):
            sci_copy(h, t, giver(t)).wait_recv()
            work(h, t)
            return carry

        lax.fori_loop(1, RES, take, 0)
        for dx in range(1, NX):
            red_copy(h, dx, x).start()

    for h in range(2):
        for dx in range(1, NX):
            red_copy(h, dx, (x + dx) % NX).wait_recv()
        total = acc[h, x]
        for dx in range(1, NX):
            total = total + part[h, (x + dx) % NX]
        for plane in range(2):
            out_ref[pl.ds(h * BLK + plane, HALF, stride=2), :] = total[plane * HALF : (plane + 1) * HALF]

    for side in (0, 1):
        edge_copy(side).wait_send()
    for dx in range(1, NX):
        sky_copy(dx, x).wait_send()
        fwd_copy(dx, x).wait_send()
        for h in range(2):
            red_copy(h, dx, x).wait_send()

    def sent(t, carry):
        tab_copy(t, r).wait_send()
        num_copy(t, r).wait_send()
        for h in range(2):
            sci_copy(h, t, r).wait_send()
        return carry

    lax.fori_loop(1, RES, sent, 0)


def per_device(science, coadd, coefficients, strip_start):
    regions = lax.axis_size("region")
    across_np, down_np, norms_np = constant_matrices()
    sci = science.reshape(2, RES, 2, BLK, CW)
    sky = coadd.reshape(2 * BLK, CW)
    coef = jnp.transpose(coefficients[0, 0], (2, 0, 1))
    starts = strip_start[0]
    dma = pltpu.SemaphoreType.DMA
    scratch = [
        pltpu.VMEM((2, RES, 2, BLK, CW), F32),
        pltpu.VMEM((2, RES, 2, BLK, CW), F32),
        pltpu.VMEM((2, RES, 2, BLK, CW), F32),
        pltpu.VMEM((NX, 2 * BLK, CW), F32),
        pltpu.VMEM((NX, 2, 2 * EDGE, CW), F32),
        pltpu.VMEM(across_np.shape, BF16),
        pltpu.VMEM(down_np.shape, BF16),
        pltpu.VMEM((2, NPROF, DEPTH, 2 * CW), BF16),
        pltpu.VMEM((NX, NBASIS, 2, HALF, CW), F32),
        pltpu.VMEM((NX, 2, HALF, CW), F32),
        pltpu.VMEM((2, NX, BLK, CW), F32),
        pltpu.VMEM((2, NX, BLK, CW), F32),
        pltpu.VMEM((8, CW), F32),
        pltpu.VMEM((RES, 8, CW), F32),
        pltpu.VMEM((8, CW), jnp.int32),
        pltpu.VMEM((RES, 8, CW), jnp.int32),
        pltpu.SMEM((RES, 8, CW), F32),
        pltpu.SMEM((RES, 8, CW), jnp.int32),
        dma((6,)),
        dma((NX,)), dma((NX,)),
        dma((2,)), dma((2,)),
        dma((NX,)), dma((NX,)),
        dma((RES,)), dma((RES,)),
        dma((RES,)), dma((RES,)),
        dma((2, RES)), dma((2, RES)),
        dma((2, NX)), dma((2, NX)),
    ]
    hbm = pl.BlockSpec(memory_space=pl.ANY)
    vmem = pl.BlockSpec(memory_space=pltpu.VMEM)
    result = pl.pallas_call(
        lambda *refs: kernel(regions, *refs),
        out_shape=jax.ShapeDtypeStruct((2 * BLK, CW), F32),
        in_specs=[hbm, hbm, vmem, pl.BlockSpec(memory_space=pltpu.SMEM), hbm, hbm, vmem],
        out_specs=vmem,
        scratch_shapes=scratch,
        compiler_params=pltpu.CompilerParams(
            collective_id=0, has_side_effects=True, vmem_limit_bytes=52 * 1024 * 1024),
        cost_estimate=pl.CostEstimate(flops=3_000_000_000, bytes_accessed=6_000_000, transcendentals=0),
        name="difference_sums",
    )(sci, sky, coef, starts, jnp.asarray(across_np), jnp.asarray(down_np), jnp.asarray(norms_np))
    return result.reshape(1, BLK, 2, CW)


def solution(mesh):
    placed = (
        P("region", "dev", None, None, None, None),
        P("region", "dev", None, None),
        P("region", "dev", None, None, None),
        P("region", "dev", None),
    )
    return jax.shard_map(
        per_device,
        mesh=mesh,
        in_specs=placed,
        out_specs=P("region", "dev", None, None),
        check_vma=False,
    )
```

```python
import jax
import jax.numpy as jnp
import ml_dtypes
import numpy as np
from jax import lax
from jax.experimental import pallas as pl
from jax.experimental.pallas import tpu as pltpu
from jax.sharding import PartitionSpec as P

BLK = 128
CW = 128
KSIZE = 21
NPROF = 12
NBASIS = 31
SPREADS = (1.0, 2.0, 4.0)
DEGREES = (4, 3, 2)

RES = 8
NX = 4
EDGE = 16
EXT = BLK + 2 * EDGE
DEPTH = 512
NQ = 4
PART = BLK // NQ
TILES = PART // 8
F32 = jnp.float32
BF16 = jnp.bfloat16
MESH = pl.DeviceIdType.MESH


def basis_list():
    listing = []
    offset = 0
    for degree in DEGREES:
        for vertical in range(degree + 1):
            for across in range(degree + 1 - vertical):
                listing.append((offset + vertical, offset + across))
        offset = offset + degree + 1
    return listing


BASIS = basis_list()


def profiles():
    half_width = (KSIZE - 1) // 2
    taps = np.arange(KSIZE, dtype=np.float64) - half_width
    rows = []
    for spread, degree in zip(SPREADS, DEGREES):
        for exponent in range(degree + 1):
            values = (taps / half_width) ** exponent * np.exp(-taps * taps / (2.0 * spread * spread))
            rows.append(values / np.abs(values).sum())
    return np.stack(rows)


def split_np(matrix):
    high = matrix.astype(np.float32).astype(ml_dtypes.bfloat16)
    low = (matrix - high.astype(np.float64)).astype(np.float32).astype(ml_dtypes.bfloat16)
    return high, low


def constant_matrices():
    half_width = (KSIZE - 1) // 2
    prof = profiles()
    wide = np.zeros((CW, NPROF, CW))
    for target in range(CW):
        for tap in range(KSIZE):
            source = target + tap - half_width
            if 0 <= source < CW:
                wide[source, :, target] = prof[:, tap]
    high, low = split_np(wide.reshape(CW, NPROF // 2, 2 * CW).transpose(1, 0, 2))
    across = np.concatenate([high, high, low], axis=1)
    tall = np.zeros((NPROF, BLK, EXT))
    for target in range(BLK):
        for tap in range(KSIZE):
            tall[:, target, (target + tap - half_width) % EXT] = prof[:, tap]
    high, low = split_np(tall)
    pad = np.zeros((NPROF, BLK, DEPTH - 3 * EXT), ml_dtypes.bfloat16)
    down = np.concatenate([high, low, high, pad], axis=2).reshape(NPROF * BLK, DEPTH)
    sums = prof.sum(axis=1)
    norms = np.zeros((8, CW), np.float32)
    for number, (vertical, horizontal) in enumerate(BASIS):
        norms[:, number] = sums[vertical] * sums[horizontal]
    return across, down, norms


def kernel(
    regions,
    sci_hbm, sky_hbm, coef_hbm, start_hbm, across_hbm, down_hbm, norm_hbm,
    out_ref,
    sci0, sci1, sci2, sci3, pack, recv, sky, edge, across, down, wide, basis, skyvar,
    acc, part, tab, tabs, num, nums, tab_s, num_s, coef_ref, start_ref, norm_ref,
    loc_sem, sky_ss, sky_rs, edge_ss, edge_rs, fwd_ss, fwd_rs,
    tab_ss, tab_rs, num_ss, num_rs, sci_ss, sci_rs, red_ss, red_rs,
):
    region = lax.axis_index("region")
    dev = lax.axis_index("dev")
    x = dev // RES
    r = dev % RES
    y = r // 2
    z = r % 2
    total_devs = regions * RES * NX
    whole = region * (RES * NX) + dev

    def order(i):
        return (3 * i) % RES

    def peer(t):
        return ((y + t // 2) % 4) * 2 + (z + t % 2) % 2

    def giver(t):
        return ((y + 4 - t // 2) % 4) * 2 + (z + t % 2) % 2

    def plane_id(res):
        return {"dev": x * RES + res}

    def line_id(dx):
        return {"dev": ((x + dx) % NX) * RES + r}

    def sky_id(step):
        other = (whole + step + total_devs) % total_devs
        return {"region": other // (RES * NX), "dev": other % (RES * NX)}

    def sci_copy(h, t, slot):
        return pltpu.make_async_remote_copy(
            src_ref=pack.at[h, t], dst_ref=recv.at[h, slot],
            send_sem=sci_ss.at[h, t], recv_sem=sci_rs.at[h, slot],
            device_id=plane_id(peer(t)), device_id_type=MESH)

    def tab_copy(t, slot):
        return pltpu.make_async_remote_copy(
            src_ref=tab, dst_ref=tabs.at[slot],
            send_sem=tab_ss.at[t], recv_sem=tab_rs.at[slot],
            device_id=plane_id(peer(t)), device_id_type=MESH)

    def num_copy(t, slot):
        return pltpu.make_async_remote_copy(
            src_ref=num, dst_ref=nums.at[slot],
            send_sem=num_ss.at[t], recv_sem=num_rs.at[slot],
            device_id=plane_id(peer(t)), device_id_type=MESH)

    def sky_copy(dx, slot):
        return pltpu.make_async_remote_copy(
            src_ref=sky.at[x], dst_ref=sky.at[slot],
            send_sem=sky_ss.at[dx], recv_sem=sky_rs.at[slot],
            device_id=line_id(dx), device_id_type=MESH)

    def fwd_copy(dx, slot):
        return pltpu.make_async_remote_copy(
            src_ref=edge.at[x], dst_ref=edge.at[slot],
            send_sem=fwd_ss.at[dx], recv_sem=fwd_rs.at[slot],
            device_id=line_id(dx), device_id_type=MESH)

    def edge_copy(side):
        rows = pl.ds(2 * (BLK - EDGE), 2 * EDGE) if side == 0 else pl.ds(0, 2 * EDGE)
        return pltpu.make_async_remote_copy(
            src_ref=sky.at[x, rows], dst_ref=edge.at[x_of(side), side],
            send_sem=edge_ss.at[side], recv_sem=edge_rs.at[side],
            device_id=sky_id(1 if side == 0 else -1), device_id_type=MESH)

    def x_of(side):
        other = (whole + (1 if side == 0 else -1) + total_devs) % total_devs
        return (other % (RES * NX)) // RES

    def edge_arrival(side):
        rows = pl.ds(2 * (BLK - EDGE), 2 * EDGE) if side == 0 else pl.ds(0, 2 * EDGE)
        return pltpu.make_async_remote_copy(
            src_ref=sky.at[x, rows], dst_ref=edge.at[x, side],
            send_sem=edge_ss.at[side], recv_sem=edge_rs.at[side],
            device_id=sky_id(1 if side == 0 else -1), device_id_type=MESH)

    def red_copy(h, dx, slot):
        return pltpu.make_async_remote_copy(
            src_ref=acc.at[h, (x + dx) % NX], dst_ref=part.at[h, slot],
            send_sem=red_ss.at[h, dx], recv_sem=red_rs.at[h, slot],
            device_id=line_id(dx), device_id_type=MESH)

    start_load = pltpu.make_async_copy(start_hbm, start_ref, loc_sem.at[6])
    start_load.start()
    coef_load = pltpu.make_async_copy(coef_hbm, coef_ref, loc_sem.at[7])
    coef_load.start()
    norm_load = pltpu.make_async_copy(norm_hbm, norm_ref, loc_sem.at[8])
    norm_load.start()
    sky_load = pltpu.make_async_copy(sky_hbm, sky.at[x], loc_sem.at[0])
    sky_load.start()
    sci = (sci0, sci1, sci2, sci3)
    sci_load = [pltpu.make_async_copy(sci_hbm.at[:, :, q], sci[q], loc_sem.at[9 + q]) for q in range(NQ)]
    for load in sci_load:
        load.start()
    across_load = pltpu.make_async_copy(across_hbm, across, loc_sem.at[2])
    across_load.start()
    down_load = pltpu.make_async_copy(down_hbm, down, loc_sem.at[3])
    down_load.start()

    barrier = pltpu.get_barrier_semaphore()

    def greet(t, carry):
        pl.semaphore_signal(barrier, inc=1, device_id=plane_id(peer(t)), device_id_type=MESH)
        return carry

    lax.fori_loop(1, RES, greet, 0)
    for dx in range(1, NX):
        pl.semaphore_signal(barrier, inc=1, device_id=line_id(dx), device_id_type=MESH)
    for step in (1, -1):
        pl.semaphore_signal(barrier, inc=1, device_id=sky_id(step), device_id_type=MESH)

    lanes = lax.broadcasted_iota(jnp.int32, (8, CW), 1)
    acc[...] = jnp.zeros(acc.shape, F32)
    for block in range(NX):
        for profile in range(NPROF):
            wide[block, profile, 3 * EXT : DEPTH, :] = jnp.zeros((DEPTH - 3 * EXT, CW), BF16)

    start_load.wait()
    coef_load.wait()
    norm_load.wait()
    tab[...] = jnp.zeros((8, CW), F32)
    for term in range(3):
        tab[2 * term : 2 * term + 2, 0:NBASIS] = coef_ref[term]
    raw = tab[...]
    weighted = jnp.sum(raw * norm_ref[...], axis=1, keepdims=True)
    tab[...] = jnp.where(lanes == NBASIS, weighted, raw)
    starts = (start_ref[0, 0], start_ref[0, 1])
    num[...] = jnp.where(lanes == 0, starts[0], starts[1])
    tabs[r] = tab[...]
    nums[r] = num[...]

    sky_load.wait()
    pl.semaphore_wait(barrier, RES - 1 + NX - 1 + 2)

    for side in (0, 1):
        edge_copy(side).start()
    for dx in range(1, NX):
        sky_copy(dx, x).start()

    def chosen(q, res, e):
        block = lax.rem(res - starts[e] + 4 * RES, RES)
        return sci[q][e, block]

    for q in range(NQ):
        sci_load[q].wait()

        def give(i, carry):
            t = order(i)
            for e in range(2):
                pack[q, t, e] = chosen(q, peer(t), e)
            sci_copy(q, t, r).start()
            return carry

        lax.fori_loop(1, RES, give, 0)
        for e in range(2):
            recv[q, r, e] = chosen(q, r, e)
        if q == 0:
            def give_tables(i, carry):
                t = order(i)
                tab_copy(t, r).start()
                num_copy(t, r).start()
                return carry

            lax.fori_loop(1, RES, give_tables, 0)
        if q == 1:
            for side in (0, 1):
                edge_arrival(side).wait_recv()
            for dx in range(1, NX):
                fwd_copy(dx, x).start()

    across_load.wait()

    def spread_across(rows, places):
        high = rows.astype(BF16)
        rest = (rows - high.astype(F32)).astype(BF16)
        lhs = jnp.concatenate([high, rest, high], axis=1)
        for tile in range(NPROF // 2):
            both = jnp.dot(lhs, across[tile], preferred_element_type=F32)
            for side in range(2):
                values = both[:, side * CW : (side + 1) * CW]
                high = values.astype(BF16)
                rest = (values - high.astype(F32)).astype(BF16)
                profile = 2 * tile + side
                for block, first, count, to in places:
                    wide[block, profile, to : to + count, :] = high[first : first + count]
                    wide[block, profile, EXT + to : EXT + to + count, :] = high[first : first + count]
                    wide[block, profile, 2 * EXT + to : 2 * EXT + to + count, :] = rest[first : first + count]

    def body_rows(block):
        for q in range(NQ):
            skyvar[block, q] = sky[block, pl.ds(q * 2 * PART + 1, PART, stride=2), :]
        return sky[block, pl.ds(0, BLK, stride=2), :]

    def smooth(pair):
        for across_profile in range(NPROF):
            users = [(k, v) for k, (v, a) in enumerate(BASIS) if a == across_profile]
            low_v = users[0][1]
            result = jnp.dot(
                down[low_v * BLK : (low_v + len(users)) * BLK, :],
                jnp.concatenate([wide[2 * pair, across_profile], wide[2 * pair + 1, across_profile]], axis=1),
                preferred_element_type=F32)
            for place, (k, v) in enumerate(users):
                for side in range(2):
                    for q in range(NQ):
                        row = place * BLK + q * PART
                        basis[2 * pair + side, k, q] = result[row : row + PART, side * CW : (side + 1) * CW]

    near = 2 * (x // 2) + 1 - x % 2
    far = 2 * (1 - x // 2)
    spread_across(body_rows(x), [(x, 0, BLK, 0)])
    sky_copy(1, near).wait_recv()
    spread_across(body_rows(near), [(near, 0, BLK, 0)])

    sky_top = (region == 0) & (r == 0)
    sky_end = (region == regions - 1) & (r == RES - 1)
    fwd_copy(1, near).wait_recv()
    for side in range(2):
        fwd_copy(1, far + side).wait_recv()
    rims = []
    for block in range(NX):
        top = edge[block, 0, pl.ds(0, EDGE, stride=2), :]
        low = edge[block, 1, pl.ds(0, EDGE, stride=2), :]
        if block == 0:
            top = jnp.where(sky_top, 0.0, top)
        if block == NX - 1:
            low = jnp.where(sky_end, 0.0, low)
        rims += [low, top]
    spread_across(
        jnp.concatenate(rims, axis=0), [(block, 2 * EDGE * block, 2 * EDGE, BLK) for block in range(NX)])
    down_load.wait()
    smooth(x // 2)
    for side in range(2):
        sky_copy(1, far + side).wait_recv()
    spread_across(
        jnp.concatenate([body_rows(far), body_rows(far + 1)], axis=0),
        [(far, 0, BLK, 0), (far + 1, BLK, BLK, 0)])
    smooth(1 - x // 2)

    def tables(t, carry):
        tab_copy(t, giver(t)).wait_recv()
        num_copy(t, giver(t)).wait_recv()
        return carry

    lax.fori_loop(1, RES, tables, 0)
    tab_move = pltpu.make_async_copy(tabs, tab_s, loc_sem.at[4])
    tab_move.start()
    num_move = pltpu.make_async_copy(nums, num_s, loc_sem.at[5])
    num_move.start()
    tab_move.wait()
    num_move.wait()

    xs = (2.0 * lanes.astype(F32) + 1.0) / CW - 1.0
    rows = (8 * lax.broadcasted_iota(jnp.int32, (TILES, 8, CW), 0)
            + lax.broadcasted_iota(jnp.int32, (TILES, 8, CW), 1)).astype(F32)
    ys_base = (2.0 * rows + 1.0) / (RES * BLK)

    def work(q, t):
        source = giver(t)
        found = []
        for e in range(2):
            start = num_s[source, 0, e]
            place = lax.rem(r - start + 4 * RES, RES)
            block = (start + place) // RES
            flat = jnp.zeros((TILES, 8, CW), F32)
            slope = jnp.zeros((TILES, 8, CW), F32)
            for k in range(NBASIS):
                image = basis[block, k, q].reshape(TILES, 8, CW)
                factor = tab_s[source, e, k] + tab_s[source, 2 + e, k] * xs
                flat = flat + factor[None] * image
                slope = slope + tab_s[source, 4 + e, k] * image
            y0 = (place * BLK + q * PART).astype(F32)
            ys = ys_base + (y0 * (2.0 / (RES * BLK)) - 1.0)
            gain = (tab_s[source, e, NBASIS] + tab_s[source, 2 + e, NBASIS] * xs)[None] + tab_s[
                source, 4 + e, NBASIS] * ys
            flux = recv[q, source, e, pl.ds(0, PART, stride=2), :].reshape(TILES, 8, CW)
            noise = recv[q, source, e, pl.ds(1, PART, stride=2), :].reshape(TILES, 8, CW)
            behind = skyvar[block, q].reshape(TILES, 8, CW)
            weight = 1.0 / (noise + gain * gain * behind)
            diff = (flux - (flat + ys * slope)) * weight
            found.append((block, diff.reshape(PART, CW), weight.reshape(PART, CW)))
        for target in range(NX):
            for plane in range(2):
                span = slice(plane * PART, (plane + 1) * PART)
                old = acc[q, target, span, :]
                for block, diff, weight in found:
                    old = old + jnp.where(block == target, weight if plane else diff, 0.0)
                acc[q, target, span, :] = old

    def finish(q):
        for dx in range(1, NX):
            red_copy(q, dx, (x + dx) % NX).wait_recv()
        total = acc[q, x]
        for dx in range(1, NX):
            total = total + part[q, (x + dx) % NX]
        for plane in range(2):
            out_ref[pl.ds(q * 2 * PART + plane, PART, stride=2), :] = total[plane * PART : (plane + 1) * PART]

    for q in range(NQ):
        work(q, 0)

        def take(i, carry):
            t = order(i)
            sci_copy(q, t, giver(t)).wait_recv()
            work(q, t)
            return carry

        lax.fori_loop(1, RES, take, 0)
        for dx in range(1, NX):
            red_copy(q, dx, x).start()
        if q > 0:
            finish(q - 1)
    finish(NQ - 1)

    for side in (0, 1):
        edge_copy(side).wait_send()
    for dx in range(1, NX):
        sky_copy(dx, x).wait_send()
        fwd_copy(dx, x).wait_send()
        for q in range(NQ):
            red_copy(q, dx, x).wait_send()

    def sent(t, carry):
        tab_copy(t, r).wait_send()
        num_copy(t, r).wait_send()
        for q in range(NQ):
            sci_copy(q, t, r).wait_send()
        return carry

    lax.fori_loop(1, RES, sent, 0)


def per_device(science, coadd, coefficients, strip_start):
    regions = lax.axis_size("region")
    across_np, down_np, norms_np = constant_matrices()
    sci = science.reshape(2, RES, NQ, 2 * PART, CW)
    sky = coadd.reshape(2 * BLK, CW)
    coef = jnp.transpose(coefficients[0, 0], (2, 0, 1))
    starts = strip_start[0]
    dma = pltpu.SemaphoreType.DMA
    scratch = [
        *[pltpu.VMEM((2, RES, 2 * PART, CW), F32) for q in range(NQ)],
        pltpu.VMEM((NQ, RES, 2, 2 * PART, CW), F32),
        pltpu.VMEM((NQ, RES, 2, 2 * PART, CW), F32),
        pltpu.VMEM((NX, 2 * BLK, CW), F32),
        pltpu.VMEM((NX, 2, 2 * EDGE, CW), F32),
        pltpu.VMEM(across_np.shape, BF16),
        pltpu.VMEM(down_np.shape, BF16),
        pltpu.VMEM((NX, NPROF, DEPTH, CW), BF16),
        pltpu.VMEM((NX, NBASIS, NQ, PART, CW), F32),
        pltpu.VMEM((NX, NQ, PART, CW), F32),
        pltpu.VMEM((NQ, NX, 2 * PART, CW), F32),
        pltpu.VMEM((NQ, NX, 2 * PART, CW), F32),
        pltpu.VMEM((8, CW), F32),
        pltpu.VMEM((RES, 8, CW), F32),
        pltpu.VMEM((8, CW), jnp.int32),
        pltpu.VMEM((RES, 8, CW), jnp.int32),
        pltpu.SMEM((RES, 8, CW), F32),
        pltpu.SMEM((RES, 8, CW), jnp.int32),
        pltpu.VMEM((3, 2, NBASIS), F32),
        pltpu.SMEM((1, 2), jnp.int32),
        pltpu.VMEM((8, CW), F32),
        dma((9 + NQ,)),
        dma((NX,)), dma((NX,)),
        dma((2,)), dma((2,)),
        dma((NX,)), dma((NX,)),
        dma((RES,)), dma((RES,)),
        dma((RES,)), dma((RES,)),
        dma((NQ, RES)), dma((NQ, RES)),
        dma((NQ, NX)), dma((NQ, NX)),
    ]
    hbm = pl.BlockSpec(memory_space=pl.ANY)
    vmem = pl.BlockSpec(memory_space=pltpu.VMEM)
    result = pl.pallas_call(
        lambda *refs: kernel(regions, *refs),
        out_shape=jax.ShapeDtypeStruct((2 * BLK, CW), F32),
        in_specs=[hbm] * 7,
        out_specs=vmem,
        scratch_shapes=scratch,
        compiler_params=pltpu.CompilerParams(
            collective_id=0, has_side_effects=True, vmem_limit_bytes=62 * 1024 * 1024),
        cost_estimate=pl.CostEstimate(flops=3_000_000_000, bytes_accessed=6_000_000, transcendentals=0),
        name="difference_sums",
    )(sci, sky, coef, starts, jnp.asarray(across_np), jnp.asarray(down_np), jnp.asarray(norms_np))
    return result.reshape(1, BLK, 2, CW)


def solution(mesh):
    placed = (
        P("region", "dev", None, None, None, None),
        P("region", "dev", None, None),
        P("region", "dev", None, None, None),
        P("region", "dev", None),
    )
    return jax.shard_map(
        per_device,
        mesh=mesh,
        in_specs=placed,
        out_specs=P("region", "dev", None, None),
        check_vma=False,
    )
```

```python
import jax
import jax.numpy as jnp
import ml_dtypes
import numpy as np
from jax import lax
from jax.experimental import pallas as pl
from jax.experimental.pallas import tpu as pltpu
from jax.sharding import PartitionSpec as P

BLK = 128
CW = 128
KSIZE = 21
NPROF = 12
NBASIS = 31
SPREADS = (1.0, 2.0, 4.0)
DEGREES = (4, 3, 2)

RES = 8
NX = 4
EDGE = 16
EXT = BLK + 2 * EDGE
DEPTH = 512
CHUNKS = (32, 32, 32, 32)
NQ = len(CHUNKS)
FIRST = tuple(sum(CHUNKS[:q]) for q in range(NQ))
F32 = jnp.float32
BF16 = jnp.bfloat16
MESH = pl.DeviceIdType.MESH


def basis_list():
    listing = []
    offset = 0
    for degree in DEGREES:
        for vertical in range(degree + 1):
            for across in range(degree + 1 - vertical):
                listing.append((offset + vertical, offset + across))
        offset = offset + degree + 1
    return listing


BASIS = basis_list()


def profiles():
    half_width = (KSIZE - 1) // 2
    taps = np.arange(KSIZE, dtype=np.float64) - half_width
    rows = []
    for spread, degree in zip(SPREADS, DEGREES):
        for exponent in range(degree + 1):
            values = (taps / half_width) ** exponent * np.exp(-taps * taps / (2.0 * spread * spread))
            rows.append(values / np.abs(values).sum())
    return np.stack(rows)


def split_np(matrix):
    high = matrix.astype(np.float32).astype(ml_dtypes.bfloat16)
    low = (matrix - high.astype(np.float64)).astype(np.float32).astype(ml_dtypes.bfloat16)
    return high, low


def constant_matrices():
    half_width = (KSIZE - 1) // 2
    prof = profiles()
    wide = np.zeros((CW, NPROF, CW))
    for target in range(CW):
        for tap in range(KSIZE):
            source = target + tap - half_width
            if 0 <= source < CW:
                wide[source, :, target] = prof[:, tap]
    high, low = split_np(wide.reshape(CW, NPROF // 2, 2 * CW).transpose(1, 0, 2))
    across = np.concatenate([high, high, low], axis=1)
    tall = np.zeros((NPROF, BLK, EXT))
    for target in range(BLK):
        for tap in range(KSIZE):
            tall[:, target, (target + tap - half_width) % EXT] = prof[:, tap]
    high, low = split_np(tall)
    pad = np.zeros((NPROF, BLK, DEPTH - 3 * EXT), ml_dtypes.bfloat16)
    down = np.concatenate([high, low, high, pad], axis=2).reshape(NPROF * BLK, DEPTH)
    sums = prof.sum(axis=1)
    norms = np.zeros((8, CW), np.float32)
    for number, (vertical, horizontal) in enumerate(BASIS):
        norms[:, number] = sums[vertical] * sums[horizontal]
    return across, down, norms


def kernel(
    regions,
    sci_hbm, sky_hbm, coef_hbm, start_hbm, across_hbm, down_hbm, norm_hbm,
    out_ref,
    sci, pack, recv, basis, skyvar, acc, part,
    sky, edge, across, down, wide, tab, tabs, num, nums, tab_s, num_s, coef_ref, start_ref, norm_ref,
    loc_sem, sky_ss, sky_rs, edge_ss, edge_rs, fwd_ss, fwd_rs,
    tab_ss, tab_rs, num_ss, num_rs, sci_ss, sci_rs, red_ss, red_rs,
):
    region = lax.axis_index("region")
    dev = lax.axis_index("dev")
    x = dev // RES
    r = dev % RES
    y = r // 2
    z = r % 2
    total_devs = regions * RES * NX
    whole = region * (RES * NX) + dev

    def order(i):
        return (3 * i) % RES

    def peer(t):
        return ((y + t // 2) % 4) * 2 + (z + t % 2) % 2

    def giver(t):
        return ((y + 4 - t // 2) % 4) * 2 + (z + t % 2) % 2

    def plane_id(res):
        return {"dev": x * RES + res}

    def line_id(dx):
        return {"dev": ((x + dx) % NX) * RES + r}

    def sky_id(step):
        other = (whole + step + total_devs) % total_devs
        return {"region": other // (RES * NX), "dev": other % (RES * NX)}

    def sci_copy(h, t, slot):
        return pltpu.make_async_remote_copy(
            src_ref=pack[h].at[t], dst_ref=recv[h].at[slot],
            send_sem=sci_ss.at[h, t], recv_sem=sci_rs.at[h, slot],
            device_id=plane_id(peer(t)), device_id_type=MESH)

    def tab_copy(t, slot):
        return pltpu.make_async_remote_copy(
            src_ref=tab, dst_ref=tabs.at[slot],
            send_sem=tab_ss.at[t], recv_sem=tab_rs.at[slot],
            device_id=plane_id(peer(t)), device_id_type=MESH)

    def num_copy(t, slot):
        return pltpu.make_async_remote_copy(
            src_ref=num, dst_ref=nums.at[slot],
            send_sem=num_ss.at[t], recv_sem=num_rs.at[slot],
            device_id=plane_id(peer(t)), device_id_type=MESH)

    def sky_copy(dx, slot):
        return pltpu.make_async_remote_copy(
            src_ref=sky.at[x], dst_ref=sky.at[slot],
            send_sem=sky_ss.at[dx], recv_sem=sky_rs.at[slot],
            device_id=line_id(dx), device_id_type=MESH)

    def fwd_copy(dx, slot):
        return pltpu.make_async_remote_copy(
            src_ref=edge.at[x], dst_ref=edge.at[slot],
            send_sem=fwd_ss.at[dx], recv_sem=fwd_rs.at[slot],
            device_id=line_id(dx), device_id_type=MESH)

    def edge_copy(side):
        rows = pl.ds(2 * (BLK - EDGE), 2 * EDGE) if side == 0 else pl.ds(0, 2 * EDGE)
        return pltpu.make_async_remote_copy(
            src_ref=sky.at[x, rows], dst_ref=edge.at[x_of(side), side],
            send_sem=edge_ss.at[side], recv_sem=edge_rs.at[side],
            device_id=sky_id(1 if side == 0 else -1), device_id_type=MESH)

    def x_of(side):
        other = (whole + (1 if side == 0 else -1) + total_devs) % total_devs
        return (other % (RES * NX)) // RES

    def edge_arrival(side):
        rows = pl.ds(2 * (BLK - EDGE), 2 * EDGE) if side == 0 else pl.ds(0, 2 * EDGE)
        return pltpu.make_async_remote_copy(
            src_ref=sky.at[x, rows], dst_ref=edge.at[x, side],
            send_sem=edge_ss.at[side], recv_sem=edge_rs.at[side],
            device_id=sky_id(1 if side == 0 else -1), device_id_type=MESH)

    def red_copy(h, dx, slot):
        return pltpu.make_async_remote_copy(
            src_ref=acc[h].at[(x + dx) % NX], dst_ref=part[h].at[slot],
            send_sem=red_ss.at[h, dx], recv_sem=red_rs.at[h, slot],
            device_id=line_id(dx), device_id_type=MESH)

    def load(source, target, number):
        copy = pltpu.make_async_copy(source, target, loc_sem.at[number])
        copy.start()
        return copy

    def load_science(q):
        rows = pl.ds(2 * FIRST[q], 2 * CHUNKS[q])
        return load(sci_hbm.at[:, :, rows], sci[q], 9 + q)

    start_load = load(start_hbm, start_ref, 6)
    sky_load = load(sky_hbm, sky.at[x], 0)
    coef_load = load(coef_hbm, coef_ref, 7)
    norm_load = load(norm_hbm, norm_ref, 8)
    sci_load = [load_science(0)]

    barrier = pltpu.get_barrier_semaphore()

    def greet(t, carry):
        pl.semaphore_signal(barrier, inc=1, device_id=plane_id(peer(t)), device_id_type=MESH)
        return carry

    lax.fori_loop(1, RES, greet, 0)
    for dx in range(1, NX):
        pl.semaphore_signal(barrier, inc=1, device_id=line_id(dx), device_id_type=MESH)
    for step in (1, -1):
        pl.semaphore_signal(barrier, inc=1, device_id=sky_id(step), device_id_type=MESH)

    sci_load += [load_science(q) for q in range(1, NQ)]
    across_load = load(across_hbm, across, 2)
    down_load = load(down_hbm, down, 3)

    lanes = lax.broadcasted_iota(jnp.int32, (8, CW), 1)
    start_load.wait()
    starts = (start_ref[0, 0], start_ref[0, 1])
    num[...] = jnp.where(lanes[0:1] == 0, starts[0], starts[1])
    coef_load.wait()
    norm_load.wait()
    tab[...] = jnp.zeros((8, CW), F32)
    for term in range(3):
        tab[2 * term : 2 * term + 2, 0:NBASIS] = coef_ref[term]
    raw = tab[...]
    weighted = jnp.sum(raw * norm_ref[...], axis=1, keepdims=True)
    tab[...] = jnp.where(lanes == NBASIS, weighted, raw)
    tabs[r] = tab[...]
    nums[r] = num[...]

    sky_load.wait()
    pl.semaphore_wait(barrier, RES - 1 + NX - 1 + 2)

    for side in (0, 1):
        edge_copy(side).start()
    for dx in range(1, NX):
        sky_copy(dx, x).start()

    def chosen(q, res, e):
        block = lax.rem(res - starts[e] + 4 * RES, RES)
        return sci[q][e, block]

    for q in range(NQ):
        sci_load[q].wait()

        def give(i, carry):
            t = order(i)
            for e in range(2):
                pack[q][t, e] = chosen(q, peer(t), e)
            sci_copy(q, t, r).start()
            return carry

        lax.fori_loop(1, RES, give, 0)
        for e in range(2):
            recv[q][r, e] = chosen(q, r, e)
        if q == 0:
            def give_tables(i, carry):
                t = order(i)
                tab_copy(t, r).start()
                num_copy(t, r).start()
                return carry

            lax.fori_loop(1, RES, give_tables, 0)
        if q == 1:
            for side in (0, 1):
                edge_arrival(side).wait_recv()
            for dx in range(1, NX):
                fwd_copy(dx, x).start()

    for q in range(NQ):
        acc[q][...] = jnp.zeros(acc[q].shape, F32)
    for block in range(NX):
        for profile in range(NPROF):
            wide[block, profile, 3 * EXT : DEPTH, :] = jnp.zeros((DEPTH - 3 * EXT, CW), BF16)
    across_load.wait()

    def spread_across(rows, places):
        high = rows.astype(BF16)
        rest = (rows - high.astype(F32)).astype(BF16)
        lhs = jnp.concatenate([high, rest, high], axis=1)
        for tile in range(NPROF // 2):
            both = jnp.dot(lhs, across[tile], preferred_element_type=F32)
            for side in range(2):
                values = both[:, side * CW : (side + 1) * CW]
                high = values.astype(BF16)
                rest = (values - high.astype(F32)).astype(BF16)
                profile = 2 * tile + side
                for block, first, count, to in places:
                    wide[block, profile, to : to + count, :] = high[first : first + count]
                    wide[block, profile, EXT + to : EXT + to + count, :] = high[first : first + count]
                    wide[block, profile, 2 * EXT + to : 2 * EXT + to + count, :] = rest[first : first + count]

    def body_rows(block):
        for q in range(NQ):
            skyvar[q][block] = sky[block, pl.ds(2 * FIRST[q] + 1, CHUNKS[q], stride=2), :]
        return sky[block, pl.ds(0, BLK, stride=2), :]

    def smooth(pair):
        for across_profile in range(NPROF):
            users = [(k, v) for k, (v, a) in enumerate(BASIS) if a == across_profile]
            low_v = users[0][1]
            result = jnp.dot(
                down[low_v * BLK : (low_v + len(users)) * BLK, :],
                jnp.concatenate([wide[2 * pair, across_profile], wide[2 * pair + 1, across_profile]], axis=1),
                preferred_element_type=F32)
            for place, (k, v) in enumerate(users):
                for side in range(2):
                    for q in range(NQ):
                        row = place * BLK + FIRST[q]
                        basis[q][2 * pair + side, k] = result[row : row + CHUNKS[q], side * CW : (side + 1) * CW]

    near = 2 * (x // 2) + 1 - x % 2
    far = 2 * (1 - x // 2)
    spread_across(body_rows(x), [(x, 0, BLK, 0)])
    sky_copy(1, near).wait_recv()
    spread_across(body_rows(near), [(near, 0, BLK, 0)])

    sky_top = (region == 0) & (r == 0)
    sky_end = (region == regions - 1) & (r == RES - 1)
    fwd_copy(1, near).wait_recv()
    for side in range(2):
        fwd_copy(1, far + side).wait_recv()
    rims = []
    for block in range(NX):
        top = edge[block, 0, pl.ds(0, EDGE, stride=2), :]
        low = edge[block, 1, pl.ds(0, EDGE, stride=2), :]
        if block == 0:
            top = jnp.where(sky_top, 0.0, top)
        if block == NX - 1:
            low = jnp.where(sky_end, 0.0, low)
        rims += [low, top]
    spread_across(
        jnp.concatenate(rims, axis=0), [(block, 2 * EDGE * block, 2 * EDGE, BLK) for block in range(NX)])
    down_load.wait()
    smooth(x // 2)
    for side in range(2):
        sky_copy(1, far + side).wait_recv()
    spread_across(
        jnp.concatenate([body_rows(far), body_rows(far + 1)], axis=0),
        [(far, 0, BLK, 0), (far + 1, BLK, BLK, 0)])
    smooth(1 - x // 2)

    def tables(t, carry):
        tab_copy(t, giver(t)).wait_recv()
        num_copy(t, giver(t)).wait_recv()
        return carry

    lax.fori_loop(1, RES, tables, 0)
    tab_move = pltpu.make_async_copy(tabs, tab_s, loc_sem.at[4])
    tab_move.start()
    num_move = pltpu.make_async_copy(nums, num_s, loc_sem.at[5])
    num_move.start()
    tab_move.wait()
    num_move.wait()

    xs = (2.0 * lanes.astype(F32) + 1.0) / CW - 1.0

    def work(q, t):
        source = giver(t)
        count = CHUNKS[q]
        shape = (count // 8, 8, CW)
        rows = (8 * lax.broadcasted_iota(jnp.int32, shape, 0) + lax.broadcasted_iota(jnp.int32, shape, 1)).astype(F32)
        ys_base = (2.0 * rows + 1.0) / (RES * BLK)
        found = []
        for e in range(2):
            start = num_s[source, 0, e]
            place = lax.rem(r - start + 4 * RES, RES)
            block = (start + place) // RES
            flat = jnp.zeros(shape, F32)
            slope = jnp.zeros(shape, F32)
            for k in range(NBASIS):
                image = basis[q][block, k].reshape(shape)
                factor = tab_s[source, e, k] + tab_s[source, 2 + e, k] * xs
                flat = flat + factor[None] * image
                slope = slope + tab_s[source, 4 + e, k] * image
            y0 = (place * BLK + FIRST[q]).astype(F32)
            ys = ys_base + (y0 * (2.0 / (RES * BLK)) - 1.0)
            gain = (tab_s[source, e, NBASIS] + tab_s[source, 2 + e, NBASIS] * xs)[None] + tab_s[
                source, 4 + e, NBASIS] * ys
            flux = recv[q][source, e, pl.ds(0, count, stride=2), :].reshape(shape)
            noise = recv[q][source, e, pl.ds(1, count, stride=2), :].reshape(shape)
            behind = skyvar[q][block].reshape(shape)
            weight = 1.0 / (noise + gain * gain * behind)
            diff = (flux - (flat + ys * slope)) * weight
            found.append((block, diff.reshape(count, CW), weight.reshape(count, CW)))
        for target in range(NX):
            for plane in range(2):
                span = slice(plane * count, (plane + 1) * count)
                old = acc[q][target, span, :]
                for block, diff, weight in found:
                    old = old + jnp.where(block == target, weight if plane else diff, 0.0)
                acc[q][target, span, :] = old

    def finish(q):
        for dx in range(1, NX):
            red_copy(q, dx, (x + dx) % NX).wait_recv()
        count = CHUNKS[q]
        total = acc[q][x]
        for dx in range(1, NX):
            total = total + part[q][(x + dx) % NX]
        for plane in range(2):
            out_ref[pl.ds(2 * FIRST[q] + plane, count, stride=2), :] = total[plane * count : (plane + 1) * count]

    for q in range(NQ):
        work(q, 0)

        def take(i, carry):
            t = order(i)
            sci_copy(q, t, giver(t)).wait_recv()
            work(q, t)
            return carry

        lax.fori_loop(1, RES, take, 0)
        for dx in range(1, NX):
            red_copy(q, dx, x).start()
        if q > 0:
            finish(q - 1)
    finish(NQ - 1)

    for side in (0, 1):
        edge_copy(side).wait_send()
    for dx in range(1, NX):
        sky_copy(dx, x).wait_send()
        fwd_copy(dx, x).wait_send()
        for q in range(NQ):
            red_copy(q, dx, x).wait_send()

    def sent(t, carry):
        tab_copy(t, r).wait_send()
        num_copy(t, r).wait_send()
        for q in range(NQ):
            sci_copy(q, t, r).wait_send()
        return carry

    lax.fori_loop(1, RES, sent, 0)


def per_device(science, coadd, coefficients, strip_start):
    regions = lax.axis_size("region")
    across_np, down_np, norms_np = constant_matrices()
    sci = science.reshape(2, RES, 2 * BLK, CW)
    sky = coadd.reshape(2 * BLK, CW)
    coef = jnp.transpose(coefficients[0, 0], (2, 0, 1))
    starts = strip_start[0]
    dma = pltpu.SemaphoreType.DMA
    def chunked(*lead):
        return [pltpu.VMEM((*lead, 2 * count, CW), F32) for count in CHUNKS]

    def single(*lead):
        return [pltpu.VMEM((*lead, count, CW), F32) for count in CHUNKS]

    scratch = [
        chunked(2, RES), chunked(RES, 2), chunked(RES, 2),
        single(NX, NBASIS), single(NX),
        chunked(NX), chunked(NX),
        pltpu.VMEM((NX, 2 * BLK, CW), F32),
        pltpu.VMEM((NX, 2, 2 * EDGE, CW), F32),
        pltpu.VMEM(across_np.shape, BF16),
        pltpu.VMEM(down_np.shape, BF16),
        pltpu.VMEM((NX, NPROF, DEPTH, CW), BF16),
        pltpu.VMEM((8, CW), F32),
        pltpu.VMEM((RES, 8, CW), F32),
        pltpu.VMEM((1, CW), jnp.int32),
        pltpu.VMEM((RES, 1, CW), jnp.int32),
        pltpu.SMEM((RES, 8, CW), F32),
        pltpu.SMEM((RES, 1, CW), jnp.int32),
        pltpu.VMEM((3, 2, NBASIS), F32),
        pltpu.SMEM((1, 2), jnp.int32),
        pltpu.VMEM((8, CW), F32),
        dma((9 + NQ,)),
        dma((NX,)), dma((NX,)),
        dma((2,)), dma((2,)),
        dma((NX,)), dma((NX,)),
        dma((RES,)), dma((RES,)),
        dma((RES,)), dma((RES,)),
        dma((NQ, RES)), dma((NQ, RES)),
        dma((NQ, NX)), dma((NQ, NX)),
    ]
    operands = (sci, sky, coef, starts, jnp.asarray(across_np), jnp.asarray(down_np), jnp.asarray(norms_np))
    hbm = pl.BlockSpec(memory_space=pl.ANY)
    vmem = pl.BlockSpec(memory_space=pltpu.VMEM)
    result = pl.pallas_call(
        lambda *refs: kernel(regions, *refs),
        out_shape=jax.ShapeDtypeStruct((2 * BLK, CW), F32),
        in_specs=[hbm] * 7,
        out_specs=vmem,
        scratch_shapes=scratch,
        compiler_params=pltpu.CompilerParams(
            collective_id=0, has_side_effects=True, vmem_limit_bytes=52 * 1024 * 1024),
        cost_estimate=pl.CostEstimate(flops=3_000_000_000, bytes_accessed=6_000_000, transcendentals=0),
        name="difference_sums",
    )(*[pltpu.with_memory_space_constraint(operand, pltpu.HBM) for operand in operands])
    return result.reshape(1, BLK, 2, CW)


def solution(mesh):
    placed = (
        P("region", "dev", None, None, None, None),
        P("region", "dev", None, None),
        P("region", "dev", None, None, None),
        P("region", "dev", None),
    )
    return jax.shard_map(
        per_device,
        mesh=mesh,
        in_specs=placed,
        out_specs=P("region", "dev", None, None),
        check_vma=False,
    )
```

```python
import jax
import jax.numpy as jnp
import ml_dtypes
import numpy as np
from jax import lax
from jax.experimental import pallas as pl
from jax.experimental.pallas import tpu as pltpu
from jax.sharding import PartitionSpec as P

BLK = 128
CW = 128
KSIZE = 21
NPROF = 12
NBASIS = 31
SPREADS = (1.0, 2.0, 4.0)
DEGREES = (4, 3, 2)

RES = 8
NX = 4
EDGE = 16
EXT = BLK + 2 * EDGE
DEPTH = 512
CHUNKS = (16, 40, 56, 16)
NQ = len(CHUNKS)
FIRST = tuple(sum(CHUNKS[:q]) for q in range(NQ))
F32 = jnp.float32
BF16 = jnp.bfloat16
MESH = pl.DeviceIdType.MESH


def basis_list():
    listing = []
    offset = 0
    for degree in DEGREES:
        for vertical in range(degree + 1):
            for across in range(degree + 1 - vertical):
                listing.append((offset + vertical, offset + across))
        offset = offset + degree + 1
    return listing


BASIS = basis_list()


def profiles():
    half_width = (KSIZE - 1) // 2
    taps = np.arange(KSIZE, dtype=np.float64) - half_width
    rows = []
    for spread, degree in zip(SPREADS, DEGREES):
        for exponent in range(degree + 1):
            values = (taps / half_width) ** exponent * np.exp(-taps * taps / (2.0 * spread * spread))
            rows.append(values / np.abs(values).sum())
    return np.stack(rows)


def split_np(matrix):
    high = matrix.astype(np.float32).astype(ml_dtypes.bfloat16)
    low = (matrix - high.astype(np.float64)).astype(np.float32).astype(ml_dtypes.bfloat16)
    return high, low


def constant_matrices():
    half_width = (KSIZE - 1) // 2
    prof = profiles()
    wide = np.zeros((CW, NPROF, CW))
    for target in range(CW):
        for tap in range(KSIZE):
            source = target + tap - half_width
            if 0 <= source < CW:
                wide[source, :, target] = prof[:, tap]
    high, low = split_np(wide.reshape(CW, NPROF // 2, 2 * CW).transpose(1, 0, 2))
    across = np.concatenate([high, high, low], axis=1)
    tall = np.zeros((NPROF, BLK, EXT))
    for target in range(BLK):
        for tap in range(KSIZE):
            tall[:, target, (target + tap - half_width) % EXT] = prof[:, tap]
    high, low = split_np(tall)
    pad = np.zeros((NPROF, BLK, DEPTH - 3 * EXT), ml_dtypes.bfloat16)
    down = np.concatenate([high, low, high, pad], axis=2).reshape(NPROF * BLK, DEPTH)
    sums = prof.sum(axis=1)
    norms = np.zeros((8, CW), np.float32)
    for number, (vertical, horizontal) in enumerate(BASIS):
        norms[:, number] = sums[vertical] * sums[horizontal]
    return across, down, norms


def kernel(
    regions,
    sci_hbm, sky_hbm, coef_hbm, start_hbm, across_hbm, down_hbm, norm_hbm,
    out_ref,
    sci, pack, recv, basis, skyvar, modelled, acc, part,
    sky, edge, across, down, wide, tab, tabs, num, nums, tab_s, num_s, coef_ref, start_ref, norm_ref,
    loc_sem, sky_ss, sky_rs, edge_ss, edge_rs, fwd_ss, fwd_rs,
    tab_ss, tab_rs, num_ss, num_rs, sci_ss, sci_rs, red_ss, red_rs,
):
    region = lax.axis_index("region")
    dev = lax.axis_index("dev")
    x = dev // RES
    r = dev % RES
    y = r // 2
    z = r % 2
    total_devs = regions * RES * NX
    whole = region * (RES * NX) + dev

    def order(i):
        return (3 * i) % RES

    def peer(t):
        return ((y + t // 2) % 4) * 2 + (z + t % 2) % 2

    def giver(t):
        return ((y + 4 - t // 2) % 4) * 2 + (z + t % 2) % 2

    def plane_id(res):
        return {"dev": x * RES + res}

    def line_id(dx):
        return {"dev": ((x + dx) % NX) * RES + r}

    def sky_id(step):
        other = (whole + step + total_devs) % total_devs
        return {"region": other // (RES * NX), "dev": other % (RES * NX)}

    def sci_copy(h, t, slot):
        return pltpu.make_async_remote_copy(
            src_ref=pack[h].at[t], dst_ref=recv[h].at[slot],
            send_sem=sci_ss.at[h, t], recv_sem=sci_rs.at[h, slot],
            device_id=plane_id(peer(t)), device_id_type=MESH)

    def tab_copy(t, slot):
        return pltpu.make_async_remote_copy(
            src_ref=tab, dst_ref=tabs.at[slot],
            send_sem=tab_ss.at[t], recv_sem=tab_rs.at[slot],
            device_id=plane_id(peer(t)), device_id_type=MESH)

    def num_copy(t, slot):
        return pltpu.make_async_remote_copy(
            src_ref=num, dst_ref=nums.at[slot],
            send_sem=num_ss.at[t], recv_sem=num_rs.at[slot],
            device_id=plane_id(peer(t)), device_id_type=MESH)

    def sky_copy(dx, slot):
        return pltpu.make_async_remote_copy(
            src_ref=sky.at[x], dst_ref=sky.at[slot],
            send_sem=sky_ss.at[dx], recv_sem=sky_rs.at[slot],
            device_id=line_id(dx), device_id_type=MESH)

    def fwd_copy(dx, slot):
        return pltpu.make_async_remote_copy(
            src_ref=edge.at[x], dst_ref=edge.at[slot],
            send_sem=fwd_ss.at[dx], recv_sem=fwd_rs.at[slot],
            device_id=line_id(dx), device_id_type=MESH)

    def edge_copy(side):
        rows = pl.ds(2 * (BLK - EDGE), 2 * EDGE) if side == 0 else pl.ds(0, 2 * EDGE)
        return pltpu.make_async_remote_copy(
            src_ref=sky.at[x, rows], dst_ref=edge.at[x_of(side), side],
            send_sem=edge_ss.at[side], recv_sem=edge_rs.at[side],
            device_id=sky_id(1 if side == 0 else -1), device_id_type=MESH)

    def x_of(side):
        other = (whole + (1 if side == 0 else -1) + total_devs) % total_devs
        return (other % (RES * NX)) // RES

    def edge_arrival(side):
        rows = pl.ds(2 * (BLK - EDGE), 2 * EDGE) if side == 0 else pl.ds(0, 2 * EDGE)
        return pltpu.make_async_remote_copy(
            src_ref=sky.at[x, rows], dst_ref=edge.at[x, side],
            send_sem=edge_ss.at[side], recv_sem=edge_rs.at[side],
            device_id=sky_id(1 if side == 0 else -1), device_id_type=MESH)

    def red_copy(h, dx, slot):
        return pltpu.make_async_remote_copy(
            src_ref=acc[h].at[(x + dx) % NX], dst_ref=part[h].at[slot],
            send_sem=red_ss.at[h, dx], recv_sem=red_rs.at[h, slot],
            device_id=line_id(dx), device_id_type=MESH)

    def load(source, target, number):
        copy = pltpu.make_async_copy(source, target, loc_sem.at[number])
        copy.start()
        return copy

    def load_science(q):
        rows = pl.ds(2 * FIRST[q], 2 * CHUNKS[q])
        return load(sci_hbm.at[:, :, rows], sci[q], 9 + q)

    start_load = load(start_hbm, start_ref, 6)
    sky_load = load(sky_hbm, sky.at[x], 0)
    coef_load = load(coef_hbm, coef_ref, 7)
    norm_load = load(norm_hbm, norm_ref, 8)
    sci_load = [load_science(0)]

    barrier = pltpu.get_barrier_semaphore()

    def greet(t, carry):
        pl.semaphore_signal(barrier, inc=1, device_id=plane_id(peer(t)), device_id_type=MESH)
        return carry

    lax.fori_loop(1, RES, greet, 0)
    for dx in range(1, NX):
        pl.semaphore_signal(barrier, inc=1, device_id=line_id(dx), device_id_type=MESH)
    for step in (1, -1):
        pl.semaphore_signal(barrier, inc=1, device_id=sky_id(step), device_id_type=MESH)

    sci_load += [load_science(q) for q in range(1, NQ)]
    across_load = load(across_hbm, across, 2)
    down_load = load(down_hbm, down, 3)

    lanes = lax.broadcasted_iota(jnp.int32, (8, CW), 1)
    start_load.wait()
    starts = (start_ref[0, 0], start_ref[0, 1])
    num[...] = jnp.where(lanes[0:1] == 0, starts[0], starts[1])
    coef_load.wait()
    norm_load.wait()
    tab[...] = jnp.zeros((8, CW), F32)
    for term in range(3):
        tab[2 * term : 2 * term + 2, 0:NBASIS] = coef_ref[term]
    raw = tab[...]
    weighted = jnp.sum(raw * norm_ref[...], axis=1, keepdims=True)
    tab[...] = jnp.where(lanes == NBASIS, weighted, raw)
    tabs[r] = tab[...]
    nums[r] = num[...]

    sky_load.wait()
    pl.semaphore_wait(barrier, RES - 1 + NX - 1 + 2)

    for side in (0, 1):
        edge_copy(side).start()
    for dx in range(1, NX):
        sky_copy(dx, x).start()

    def chosen(q, res, e):
        block = lax.rem(res - starts[e] + 4 * RES, RES)
        return sci[q][e, block]

    for q in range(NQ):
        sci_load[q].wait()

        def give(i, carry):
            t = order(i)
            for e in range(2):
                pack[q][t, e] = chosen(q, peer(t), e)
            sci_copy(q, t, r).start()
            return carry

        lax.fori_loop(1, RES, give, 0)
        for e in range(2):
            recv[q][r, e] = chosen(q, r, e)
        if q == 0:
            def give_tables(i, carry):
                t = order(i)
                tab_copy(t, r).start()
                num_copy(t, r).start()
                return carry

            lax.fori_loop(1, RES, give_tables, 0)
        if q == 1:
            for side in (0, 1):
                edge_arrival(side).wait_recv()
            for dx in range(1, NX):
                fwd_copy(dx, x).start()

    for q in range(NQ):
        acc[q][...] = jnp.zeros(acc[q].shape, F32)
    for block in range(NX):
        for profile in range(NPROF):
            wide[block, profile, 3 * EXT : DEPTH, :] = jnp.zeros((DEPTH - 3 * EXT, CW), BF16)
    across_load.wait()

    def spread_across(rows, places):
        high = rows.astype(BF16)
        rest = (rows - high.astype(F32)).astype(BF16)
        lhs = jnp.concatenate([high, rest, high], axis=1)
        for tile in range(NPROF // 2):
            both = jnp.dot(lhs, across[tile], preferred_element_type=F32)
            for side in range(2):
                values = both[:, side * CW : (side + 1) * CW]
                high = values.astype(BF16)
                rest = (values - high.astype(F32)).astype(BF16)
                profile = 2 * tile + side
                for block, first, count, to in places:
                    wide[block, profile, to : to + count, :] = high[first : first + count]
                    wide[block, profile, EXT + to : EXT + to + count, :] = high[first : first + count]
                    wide[block, profile, 2 * EXT + to : 2 * EXT + to + count, :] = rest[first : first + count]

    def body_rows(block):
        for q in range(NQ):
            skyvar[q][block] = sky[block, pl.ds(2 * FIRST[q] + 1, CHUNKS[q], stride=2), :]
        return sky[block, pl.ds(0, BLK, stride=2), :]

    def smooth(pair):
        for across_profile in range(NPROF):
            users = [(k, v) for k, (v, a) in enumerate(BASIS) if a == across_profile]
            low_v = users[0][1]
            result = jnp.dot(
                down[low_v * BLK : (low_v + len(users)) * BLK, :],
                jnp.concatenate([wide[2 * pair, across_profile], wide[2 * pair + 1, across_profile]], axis=1),
                preferred_element_type=F32)
            for place, (k, v) in enumerate(users):
                for side in range(2):
                    for q in range(NQ):
                        row = place * BLK + FIRST[q]
                        basis[q][2 * pair + side, k] = result[row : row + CHUNKS[q], side * CW : (side + 1) * CW]

    near = 2 * (x // 2) + 1 - x % 2
    far = 2 * (1 - x // 2)
    spread_across(body_rows(x), [(x, 0, BLK, 0)])
    sky_copy(1, near).wait_recv()
    spread_across(body_rows(near), [(near, 0, BLK, 0)])

    sky_top = (region == 0) & (r == 0)
    sky_end = (region == regions - 1) & (r == RES - 1)
    fwd_copy(1, near).wait_recv()
    for side in range(2):
        fwd_copy(1, far + side).wait_recv()
    rims = []
    for block in range(NX):
        top = edge[block, 0, pl.ds(0, EDGE, stride=2), :]
        low = edge[block, 1, pl.ds(0, EDGE, stride=2), :]
        if block == 0:
            top = jnp.where(sky_top, 0.0, top)
        if block == NX - 1:
            low = jnp.where(sky_end, 0.0, low)
        rims += [low, top]
    spread_across(
        jnp.concatenate(rims, axis=0), [(block, 2 * EDGE * block, 2 * EDGE, BLK) for block in range(NX)])
    down_load.wait()
    smooth(x // 2)
    for side in range(2):
        sky_copy(1, far + side).wait_recv()
    spread_across(
        jnp.concatenate([body_rows(far), body_rows(far + 1)], axis=0),
        [(far, 0, BLK, 0), (far + 1, BLK, BLK, 0)])
    smooth(1 - x // 2)

    def tables(t, carry):
        tab_copy(t, giver(t)).wait_recv()
        num_copy(t, giver(t)).wait_recv()
        return carry

    lax.fori_loop(1, RES, tables, 0)
    tab_move = pltpu.make_async_copy(tabs, tab_s, loc_sem.at[4])
    tab_move.start()
    num_move = pltpu.make_async_copy(nums, num_s, loc_sem.at[5])
    num_move.start()
    tab_move.wait()
    num_move.wait()

    xs = (2.0 * lanes.astype(F32) + 1.0) / CW - 1.0

    def model(q, t):
        source = giver(t)
        shape = (CHUNKS[q] // 8, 8, CW)
        rows = (8 * lax.broadcasted_iota(jnp.int32, shape, 0) + lax.broadcasted_iota(jnp.int32, shape, 1)).astype(F32)
        ys_base = (2.0 * rows + 1.0) / (RES * BLK)
        for e in range(2):
            start = num_s[source, 0, e]
            place = lax.rem(r - start + 4 * RES, RES)
            block = (start + place) // RES
            flat = jnp.zeros(shape, F32)
            slope = jnp.zeros(shape, F32)
            for k in range(NBASIS):
                image = basis[q][block, k].reshape(shape)
                factor = tab_s[source, e, k] + tab_s[source, 2 + e, k] * xs
                flat = flat + factor[None] * image
                slope = slope + tab_s[source, 4 + e, k] * image
            y0 = (place * BLK + FIRST[q]).astype(F32)
            ys = ys_base + (y0 * (2.0 / (RES * BLK)) - 1.0)
            gain = (tab_s[source, e, NBASIS] + tab_s[source, 2 + e, NBASIS] * xs)[None] + tab_s[
                source, 4 + e, NBASIS] * ys
            behind = skyvar[q][block].reshape(shape)
            modelled[q][source, e, 0] = (flat + ys * slope).reshape(CHUNKS[q], CW)
            modelled[q][source, e, 1] = (gain * gain * behind).reshape(CHUNKS[q], CW)

    def add(q, t):
        source = giver(t)
        count = CHUNKS[q]
        found = []
        for e in range(2):
            start = num_s[source, 0, e]
            block = (start + lax.rem(r - start + 4 * RES, RES)) // RES
            flux = recv[q][source, e, pl.ds(0, count, stride=2), :]
            noise = recv[q][source, e, pl.ds(1, count, stride=2), :]
            weight = 1.0 / (noise + modelled[q][source, e, 1])
            found.append((block, (flux - modelled[q][source, e, 0]) * weight, weight))
        for target in range(NX):
            for plane in range(2):
                span = slice(plane * count, (plane + 1) * count)
                old = acc[q][target, span, :]
                for block, diff, weight in found:
                    old = old + jnp.where(block == target, weight if plane else diff, 0.0)
                acc[q][target, span, :] = old

    def finish(q):
        for dx in range(1, NX):
            red_copy(q, dx, (x + dx) % NX).wait_recv()
        count = CHUNKS[q]
        total = acc[q][x]
        for dx in range(1, NX):
            total = total + part[q][(x + dx) % NX]
        for plane in range(2):
            out_ref[pl.ds(2 * FIRST[q] + plane, count, stride=2), :] = total[plane * count : (plane + 1) * count]

    for q in range(NQ):
        def prepare(t, carry):
            model(q, t)
            return carry

        lax.fori_loop(0, RES, prepare, 0)
        add(q, 0)

        def take(i, carry):
            t = order(i)
            sci_copy(q, t, giver(t)).wait_recv()
            add(q, t)
            return carry

        lax.fori_loop(1, RES, take, 0)
        for dx in range(1, NX):
            red_copy(q, dx, x).start()
        if q > 0:
            finish(q - 1)
    finish(NQ - 1)

    for side in (0, 1):
        edge_copy(side).wait_send()
    for dx in range(1, NX):
        sky_copy(dx, x).wait_send()
        fwd_copy(dx, x).wait_send()
        for q in range(NQ):
            red_copy(q, dx, x).wait_send()

    def sent(t, carry):
        tab_copy(t, r).wait_send()
        num_copy(t, r).wait_send()
        for q in range(NQ):
            sci_copy(q, t, r).wait_send()
        return carry

    lax.fori_loop(1, RES, sent, 0)


def per_device(science, coadd, coefficients, strip_start):
    regions = lax.axis_size("region")
    across_np, down_np, norms_np = constant_matrices()
    sci = science.reshape(2, RES, 2 * BLK, CW)
    sky = coadd.reshape(2 * BLK, CW)
    coef = jnp.transpose(coefficients[0, 0], (2, 0, 1))
    starts = strip_start[0]
    dma = pltpu.SemaphoreType.DMA
    def chunked(*lead):
        return [pltpu.VMEM((*lead, 2 * count, CW), F32) for count in CHUNKS]

    def single(*lead):
        return [pltpu.VMEM((*lead, count, CW), F32) for count in CHUNKS]

    scratch = [
        chunked(2, RES), chunked(RES, 2), chunked(RES, 2),
        single(NX, NBASIS), single(NX), single(RES, 2, 2),
        chunked(NX), chunked(NX),
        pltpu.VMEM((NX, 2 * BLK, CW), F32),
        pltpu.VMEM((NX, 2, 2 * EDGE, CW), F32),
        pltpu.VMEM(across_np.shape, BF16),
        pltpu.VMEM(down_np.shape, BF16),
        pltpu.VMEM((NX, NPROF, DEPTH, CW), BF16),
        pltpu.VMEM((8, CW), F32),
        pltpu.VMEM((RES, 8, CW), F32),
        pltpu.VMEM((1, CW), jnp.int32),
        pltpu.VMEM((RES, 1, CW), jnp.int32),
        pltpu.SMEM((RES, 8, CW), F32),
        pltpu.SMEM((RES, 1, CW), jnp.int32),
        pltpu.VMEM((3, 2, NBASIS), F32),
        pltpu.SMEM((1, 2), jnp.int32),
        pltpu.VMEM((8, CW), F32),
        dma((9 + NQ,)),
        dma((NX,)), dma((NX,)),
        dma((2,)), dma((2,)),
        dma((NX,)), dma((NX,)),
        dma((RES,)), dma((RES,)),
        dma((RES,)), dma((RES,)),
        dma((NQ, RES)), dma((NQ, RES)),
        dma((NQ, NX)), dma((NQ, NX)),
    ]
    operands = (sci, sky, coef, starts, jnp.asarray(across_np), jnp.asarray(down_np), jnp.asarray(norms_np))
    hbm = pl.BlockSpec(memory_space=pl.ANY)
    vmem = pl.BlockSpec(memory_space=pltpu.VMEM)
    result = pl.pallas_call(
        lambda *refs: kernel(regions, *refs),
        out_shape=jax.ShapeDtypeStruct((2 * BLK, CW), F32),
        in_specs=[hbm] * 7,
        out_specs=vmem,
        scratch_shapes=scratch,
        compiler_params=pltpu.CompilerParams(
            collective_id=0, has_side_effects=True, vmem_limit_bytes=52 * 1024 * 1024),
        cost_estimate=pl.CostEstimate(flops=3_000_000_000, bytes_accessed=6_000_000, transcendentals=0),
        name="difference_sums",
    )(*[pltpu.with_memory_space_constraint(operand, pltpu.HBM) for operand in operands])
    return result.reshape(1, BLK, 2, CW)


def solution(mesh):
    placed = (
        P("region", "dev", None, None, None, None),
        P("region", "dev", None, None),
        P("region", "dev", None, None, None),
        P("region", "dev", None),
    )
    return jax.shard_map(
        per_device,
        mesh=mesh,
        in_specs=placed,
        out_specs=P("region", "dev", None, None),
        check_vma=False,
    )
```

```python
import jax
import jax.numpy as jnp
import ml_dtypes
import numpy as np
from jax import lax
from jax.experimental import pallas as pl
from jax.experimental.pallas import tpu as pltpu
from jax.sharding import PartitionSpec as P

BLK = 128
CW = 128
KSIZE = 21
NPROF = 12
NBASIS = 31
SPREADS = (1.0, 2.0, 4.0)
DEGREES = (4, 3, 2)

RES = 8
NX = 4
EDGE = 16
EXT = BLK + 2 * EDGE
DEPTH = 512
CHUNKS = (16, 48, 48, 16)
NQ = len(CHUNKS)
FIRST = tuple(sum(CHUNKS[:q]) for q in range(NQ))
F32 = jnp.float32
BF16 = jnp.bfloat16
MESH = pl.DeviceIdType.MESH


def basis_list():
    listing = []
    offset = 0
    for degree in DEGREES:
        for vertical in range(degree + 1):
            for across in range(degree + 1 - vertical):
                listing.append((offset + vertical, offset + across))
        offset = offset + degree + 1
    return listing


BASIS = basis_list()


def profiles():
    half_width = (KSIZE - 1) // 2
    taps = np.arange(KSIZE, dtype=np.float64) - half_width
    rows = []
    for spread, degree in zip(SPREADS, DEGREES):
        for exponent in range(degree + 1):
            values = (taps / half_width) ** exponent * np.exp(-taps * taps / (2.0 * spread * spread))
            rows.append(values / np.abs(values).sum())
    return np.stack(rows)


def split_np(matrix):
    high = matrix.astype(np.float32).astype(ml_dtypes.bfloat16)
    low = (matrix - high.astype(np.float64)).astype(np.float32).astype(ml_dtypes.bfloat16)
    return high, low


def constant_matrices():
    half_width = (KSIZE - 1) // 2
    prof = profiles()
    wide = np.zeros((CW, NPROF, CW))
    for target in range(CW):
        for tap in range(KSIZE):
            source = target + tap - half_width
            if 0 <= source < CW:
                wide[source, :, target] = prof[:, tap]
    high, low = split_np(wide.reshape(CW, NPROF // 2, 2 * CW).transpose(1, 0, 2))
    across = np.concatenate([high, high, low], axis=1)
    tall = np.zeros((NPROF, BLK, EXT))
    for target in range(BLK):
        for tap in range(KSIZE):
            tall[:, target, (target + tap - half_width) % EXT] = prof[:, tap]
    high, low = split_np(tall)
    pad = np.zeros((NPROF, BLK, DEPTH - 3 * EXT), ml_dtypes.bfloat16)
    down = np.concatenate([high, low, high, pad], axis=2).reshape(NPROF * BLK, DEPTH)
    sums = prof.sum(axis=1)
    norms = np.zeros((8, CW), np.float32)
    for number, (vertical, horizontal) in enumerate(BASIS):
        norms[:, number] = sums[vertical] * sums[horizontal]
    return across, down, norms


def kernel(
    regions,
    sci_hbm, sky_hbm, coef_hbm, start_hbm, across_hbm, down_hbm, norm_hbm,
    out_ref,
    sci, pack, recv, basis, skyvar, modelled, acc, part,
    sky, edge, across, down, wide, tab, tabs, num, nums, tab_s, num_s, coef_ref, start_ref, norm_ref,
    loc_sem, sky_ss, sky_rs, edge_ss, edge_rs, fwd_ss, fwd_rs,
    tab_ss, tab_rs, num_ss, num_rs, sci_ss, sci_rs, red_ss, red_rs,
):
    region = lax.axis_index("region")
    dev = lax.axis_index("dev")
    x = dev // RES
    r = dev % RES
    y = r // 2
    z = r % 2
    total_devs = regions * RES * NX
    whole = region * (RES * NX) + dev

    def order(i):
        return (lax.shift_right_logical(jnp.int32(15394568), jnp.int32(3 * i)) % RES)

    def peer(t):
        return ((y + t // 2) % 4) * 2 + (z + t % 2) % 2

    def giver(t):
        return ((y + 4 - t // 2) % 4) * 2 + (z + t % 2) % 2

    def plane_id(res):
        return {"dev": x * RES + res}

    def line_id(dx):
        return {"dev": ((x + dx) % NX) * RES + r}

    def sky_id(step):
        other = (whole + step + total_devs) % total_devs
        return {"region": other // (RES * NX), "dev": other % (RES * NX)}

    def sci_copy(h, t, slot):
        return pltpu.make_async_remote_copy(
            src_ref=pack[h].at[t], dst_ref=recv[h].at[slot],
            send_sem=sci_ss.at[h, t], recv_sem=sci_rs.at[h, slot],
            device_id=plane_id(peer(t)), device_id_type=MESH)

    def tab_copy(t, slot):
        return pltpu.make_async_remote_copy(
            src_ref=tab, dst_ref=tabs.at[slot],
            send_sem=tab_ss.at[t], recv_sem=tab_rs.at[slot],
            device_id=plane_id(peer(t)), device_id_type=MESH)

    def num_copy(t, slot):
        return pltpu.make_async_remote_copy(
            src_ref=num, dst_ref=nums.at[slot],
            send_sem=num_ss.at[t], recv_sem=num_rs.at[slot],
            device_id=plane_id(peer(t)), device_id_type=MESH)

    def sky_copy(dx, slot):
        return pltpu.make_async_remote_copy(
            src_ref=sky.at[x], dst_ref=sky.at[slot],
            send_sem=sky_ss.at[dx], recv_sem=sky_rs.at[slot],
            device_id=line_id(dx), device_id_type=MESH)

    def fwd_copy(dx, slot):
        return pltpu.make_async_remote_copy(
            src_ref=edge.at[x], dst_ref=edge.at[slot],
            send_sem=fwd_ss.at[dx], recv_sem=fwd_rs.at[slot],
            device_id=line_id(dx), device_id_type=MESH)

    def edge_copy(side):
        rows = pl.ds(2 * (BLK - EDGE), 2 * EDGE) if side == 0 else pl.ds(0, 2 * EDGE)
        return pltpu.make_async_remote_copy(
            src_ref=sky.at[x, rows], dst_ref=edge.at[x_of(side), side],
            send_sem=edge_ss.at[side], recv_sem=edge_rs.at[side],
            device_id=sky_id(1 if side == 0 else -1), device_id_type=MESH)

    def x_of(side):
        other = (whole + (1 if side == 0 else -1) + total_devs) % total_devs
        return (other % (RES * NX)) // RES

    def edge_arrival(side):
        rows = pl.ds(2 * (BLK - EDGE), 2 * EDGE) if side == 0 else pl.ds(0, 2 * EDGE)
        return pltpu.make_async_remote_copy(
            src_ref=sky.at[x, rows], dst_ref=edge.at[x, side],
            send_sem=edge_ss.at[side], recv_sem=edge_rs.at[side],
            device_id=sky_id(1 if side == 0 else -1), device_id_type=MESH)

    def red_copy(h, dx, slot):
        return pltpu.make_async_remote_copy(
            src_ref=acc[h].at[(x + dx) % NX], dst_ref=part[h].at[slot],
            send_sem=red_ss.at[h, dx], recv_sem=red_rs.at[h, slot],
            device_id=line_id(dx), device_id_type=MESH)

    def load(source, target, number):
        copy = pltpu.make_async_copy(source, target, loc_sem.at[number])
        copy.start()
        return copy

    def load_science(q):
        rows = pl.ds(2 * FIRST[q], 2 * CHUNKS[q])
        return load(sci_hbm.at[:, :, rows], sci[q], 9 + q)

    start_load = load(start_hbm, start_ref, 6)
    sky_load = load(sky_hbm, sky.at[x], 0)
    coef_load = load(coef_hbm, coef_ref, 7)
    norm_load = load(norm_hbm, norm_ref, 8)
    sci_load = [load_science(0)]

    barrier = pltpu.get_barrier_semaphore()

    def greet(t, carry):
        pl.semaphore_signal(barrier, inc=1, device_id=plane_id(peer(t)), device_id_type=MESH)
        return carry

    lax.fori_loop(1, RES, greet, 0)
    for dx in range(1, NX):
        pl.semaphore_signal(barrier, inc=1, device_id=line_id(dx), device_id_type=MESH)

    has_next = whole < total_devs - 1
    has_previous = whole > 0
    for step, there in ((1, has_next), (-1, has_previous)):
        @pl.when(there)
        def _():
            pl.semaphore_signal(barrier, inc=1, device_id=sky_id(step), device_id_type=MESH)

    sci_load += [load_science(q) for q in range(1, NQ)]
    across_load = load(across_hbm, across, 2)
    down_load = load(down_hbm, down, 3)

    lanes = lax.broadcasted_iota(jnp.int32, (8, CW), 1)
    start_load.wait()
    starts = (start_ref[0, 0], start_ref[0, 1])
    num[...] = jnp.where(lanes[0:1] == 0, starts[0], starts[1])
    sky_load.wait()
    ends = (whole + total_devs - 1) // total_devs + (2 * total_devs - 2 - whole) // total_devs
    pl.semaphore_wait(barrier, RES - 1 + NX - 1 + ends)

    for side, there in ((0, has_next), (1, has_previous)):
        @pl.when(there)
        def _():
            edge_copy(side).start()
    for dx in range(1, NX):
        sky_copy(dx, x).start()

    def chosen(q, res, e):
        block = lax.rem(res - starts[e] + 4 * RES, RES)
        return sci[q][e, block]

    for q in range(NQ):
        sci_load[q].wait()

        def give(i, carry):
            t = order(i)
            for e in range(2):
                pack[q][t, e] = chosen(q, peer(t), e)
            sci_copy(q, t, r).start()
            return carry

        lax.fori_loop(1, RES, give, 0)
        for e in range(2):
            recv[q][r, e] = chosen(q, r, e)
        if q == 0:
            coef_load.wait()
            norm_load.wait()
            tab[...] = jnp.zeros((8, CW), F32)
            for term in range(3):
                tab[2 * term : 2 * term + 2, 0:NBASIS] = coef_ref[term]
            raw = tab[...]
            weighted = jnp.sum(raw * norm_ref[...], axis=1, keepdims=True)
            tab[...] = jnp.where(lanes == NBASIS, weighted, raw)
            tabs[r] = tab[...]
            nums[r] = num[...]

            def give_tables(i, carry):
                t = order(i)
                tab_copy(t, r).start()
                num_copy(t, r).start()
                return carry

            lax.fori_loop(1, RES, give_tables, 0)
        if q == 1:
            for side, there in ((0, has_previous), (1, has_next)):
                @pl.when(there)
                def _():
                    edge_arrival(side).wait_recv()

                @pl.when(jnp.logical_not(there))
                def _():
                    edge[x, side] = jnp.zeros((2 * EDGE, CW), F32)
            for dx in range(1, NX):
                fwd_copy(dx, x).start()

    for q in range(NQ):
        acc[q][...] = jnp.zeros(acc[q].shape, F32)
    for block in range(NX):
        for profile in range(NPROF):
            wide[block, profile, 3 * EXT : DEPTH, :] = jnp.zeros((DEPTH - 3 * EXT, CW), BF16)
    across_load.wait()

    def spread_across(rows, places):
        high = rows.astype(BF16)
        rest = (rows - high.astype(F32)).astype(BF16)
        lhs = jnp.concatenate([high, rest, high], axis=1)
        for tile in range(NPROF // 2):
            both = jnp.dot(lhs, across[tile], preferred_element_type=F32)
            for side in range(2):
                values = both[:, side * CW : (side + 1) * CW]
                high = values.astype(BF16)
                rest = (values - high.astype(F32)).astype(BF16)
                profile = 2 * tile + side
                for block, first, count, to in places:
                    wide[block, profile, to : to + count, :] = high[first : first + count]
                    wide[block, profile, EXT + to : EXT + to + count, :] = high[first : first + count]
                    wide[block, profile, 2 * EXT + to : 2 * EXT + to + count, :] = rest[first : first + count]

    def body_rows(block):
        for q in range(NQ):
            skyvar[q][block] = sky[block, pl.ds(2 * FIRST[q] + 1, CHUNKS[q], stride=2), :]
        return sky[block, pl.ds(0, BLK, stride=2), :]

    def smooth(pair):
        for across_profile in range(NPROF):
            users = [(k, v) for k, (v, a) in enumerate(BASIS) if a == across_profile]
            low_v = users[0][1]
            result = jnp.dot(
                down[low_v * BLK : (low_v + len(users)) * BLK, :],
                jnp.concatenate([wide[2 * pair, across_profile], wide[2 * pair + 1, across_profile]], axis=1),
                preferred_element_type=F32)
            for place, (k, v) in enumerate(users):
                for side in range(2):
                    for q in range(NQ):
                        row = place * BLK + FIRST[q]
                        basis[q][2 * pair + side, k] = result[row : row + CHUNKS[q], side * CW : (side + 1) * CW]

    near = 2 * (x // 2) + 1 - x % 2
    far = 2 * (1 - x // 2)
    spread_across(body_rows(x), [(x, 0, BLK, 0)])
    sky_copy(1, near).wait_recv()
    spread_across(body_rows(near), [(near, 0, BLK, 0)])

    fwd_copy(1, near).wait_recv()
    for side in range(2):
        fwd_copy(1, far + side).wait_recv()
    rims = []
    for block in range(NX):
        top = edge[block, 0, pl.ds(0, EDGE, stride=2), :]
        low = edge[block, 1, pl.ds(0, EDGE, stride=2), :]
        rims += [low, top]
    spread_across(
        jnp.concatenate(rims, axis=0), [(block, 2 * EDGE * block, 2 * EDGE, BLK) for block in range(NX)])
    down_load.wait()
    smooth(x // 2)
    for side in range(2):
        sky_copy(1, far + side).wait_recv()
    spread_across(
        jnp.concatenate([body_rows(far), body_rows(far + 1)], axis=0),
        [(far, 0, BLK, 0), (far + 1, BLK, BLK, 0)])
    smooth(1 - x // 2)

    def tables(t, carry):
        tab_copy(t, giver(t)).wait_recv()
        num_copy(t, giver(t)).wait_recv()
        return carry

    lax.fori_loop(1, RES, tables, 0)
    tab_move = pltpu.make_async_copy(tabs, tab_s, loc_sem.at[4])
    tab_move.start()
    num_move = pltpu.make_async_copy(nums, num_s, loc_sem.at[5])
    num_move.start()
    tab_move.wait()
    num_move.wait()

    xs = (2.0 * lanes.astype(F32) + 1.0) / CW - 1.0

    def model(q, t):
        source = giver(t)
        shape = (CHUNKS[q] // 8, 8, CW)
        rows = (8 * lax.broadcasted_iota(jnp.int32, shape, 0) + lax.broadcasted_iota(jnp.int32, shape, 1)).astype(F32)
        ys_base = (2.0 * rows + 1.0) / (RES * BLK)
        for e in range(2):
            start = num_s[source, 0, e]
            place = lax.rem(r - start + 4 * RES, RES)
            block = (start + place) // RES
            flat = jnp.zeros(shape, F32)
            slope = jnp.zeros(shape, F32)
            for k in range(NBASIS):
                image = basis[q][block, k].reshape(shape)
                factor = tab_s[source, e, k] + tab_s[source, 2 + e, k] * xs
                flat = flat + factor[None] * image
                slope = slope + tab_s[source, 4 + e, k] * image
            y0 = (place * BLK + FIRST[q]).astype(F32)
            ys = ys_base + (y0 * (2.0 / (RES * BLK)) - 1.0)
            gain = (tab_s[source, e, NBASIS] + tab_s[source, 2 + e, NBASIS] * xs)[None] + tab_s[
                source, 4 + e, NBASIS] * ys
            behind = skyvar[q][block].reshape(shape)
            modelled[q][source, e, 0] = (flat + ys * slope).reshape(CHUNKS[q], CW)
            modelled[q][source, e, 1] = (gain * gain * behind).reshape(CHUNKS[q], CW)

    def add(q, t):
        source = giver(t)
        count = CHUNKS[q]
        found = []
        for e in range(2):
            start = num_s[source, 0, e]
            block = (start + lax.rem(r - start + 4 * RES, RES)) // RES
            flux = recv[q][source, e, pl.ds(0, count, stride=2), :]
            noise = recv[q][source, e, pl.ds(1, count, stride=2), :]
            weight = 1.0 / (noise + modelled[q][source, e, 1])
            found.append((block, (flux - modelled[q][source, e, 0]) * weight, weight))
        for target in range(NX):
            for plane in range(2):
                span = slice(plane * count, (plane + 1) * count)
                old = acc[q][target, span, :]
                for block, diff, weight in found:
                    old = old + jnp.where(block == target, weight if plane else diff, 0.0)
                acc[q][target, span, :] = old

    def finish(q):
        for dx in range(1, NX):
            red_copy(q, dx, (x + dx) % NX).wait_recv()
        count = CHUNKS[q]
        total = acc[q][x]
        for dx in range(1, NX):
            total = total + part[q][(x + dx) % NX]
        for plane in range(2):
            out_ref[pl.ds(2 * FIRST[q] + plane, count, stride=2), :] = total[plane * count : (plane + 1) * count]

    for q in range(NQ):
        def prepare(t, carry):
            model(q, t)
            return carry

        lax.fori_loop(0, RES, prepare, 0)
        add(q, 0)

        def take(i, carry):
            t = order(i)
            sci_copy(q, t, giver(t)).wait_recv()
            add(q, t)
            return carry

        lax.fori_loop(1, RES, take, 0)
        for dx in range(1, NX):
            red_copy(q, dx, x).start()
        if q > 0:
            finish(q - 1)
    finish(NQ - 1)

    for side, there in ((0, has_next), (1, has_previous)):
        @pl.when(there)
        def _():
            edge_copy(side).wait_send()
    for dx in range(1, NX):
        sky_copy(dx, x).wait_send()
        fwd_copy(dx, x).wait_send()
        for q in range(NQ):
            red_copy(q, dx, x).wait_send()

    def sent(t, carry):
        tab_copy(t, r).wait_send()
        num_copy(t, r).wait_send()
        for q in range(NQ):
            sci_copy(q, t, r).wait_send()
        return carry

    lax.fori_loop(1, RES, sent, 0)


def per_device(science, coadd, coefficients, strip_start):
    regions = lax.axis_size("region")
    across_np, down_np, norms_np = constant_matrices()
    sci = science.reshape(2, RES, 2 * BLK, CW)
    sky = coadd.reshape(2 * BLK, CW)
    coef = jnp.transpose(coefficients[0, 0], (2, 0, 1))
    starts = strip_start[0]
    dma = pltpu.SemaphoreType.DMA
    def chunked(*lead):
        return [pltpu.VMEM((*lead, 2 * count, CW), F32) for count in CHUNKS]

    def single(*lead):
        return [pltpu.VMEM((*lead, count, CW), F32) for count in CHUNKS]

    scratch = [
        chunked(2, RES), chunked(RES, 2), chunked(RES, 2),
        single(NX, NBASIS), single(NX), single(RES, 2, 2),
        chunked(NX), chunked(NX),
        pltpu.VMEM((NX, 2 * BLK, CW), F32),
        pltpu.VMEM((NX, 2, 2 * EDGE, CW), F32),
        pltpu.VMEM(across_np.shape, BF16),
        pltpu.VMEM(down_np.shape, BF16),
        pltpu.VMEM((NX, NPROF, DEPTH, CW), BF16),
        pltpu.VMEM((8, CW), F32),
        pltpu.VMEM((RES, 8, CW), F32),
        pltpu.VMEM((1, CW), jnp.int32),
        pltpu.VMEM((RES, 1, CW), jnp.int32),
        pltpu.SMEM((RES, 8, CW), F32),
        pltpu.SMEM((RES, 1, CW), jnp.int32),
        pltpu.VMEM((3, 2, NBASIS), F32),
        pltpu.SMEM((1, 2), jnp.int32),
        pltpu.VMEM((8, CW), F32),
        dma((9 + NQ,)),
        dma((NX,)), dma((NX,)),
        dma((2,)), dma((2,)),
        dma((NX,)), dma((NX,)),
        dma((RES,)), dma((RES,)),
        dma((RES,)), dma((RES,)),
        dma((NQ, RES)), dma((NQ, RES)),
        dma((NQ, NX)), dma((NQ, NX)),
    ]
    operands = (sci, sky, coef, starts, jnp.asarray(across_np), jnp.asarray(down_np), jnp.asarray(norms_np))
    hbm = pl.BlockSpec(memory_space=pl.ANY)
    vmem = pl.BlockSpec(memory_space=pltpu.VMEM)
    result = pl.pallas_call(
        lambda *refs: kernel(regions, *refs),
        out_shape=jax.ShapeDtypeStruct((2 * BLK, CW), F32),
        in_specs=[hbm] * 7,
        out_specs=vmem,
        scratch_shapes=scratch,
        compiler_params=pltpu.CompilerParams(
            collective_id=0, has_side_effects=True, vmem_limit_bytes=52 * 1024 * 1024),
        cost_estimate=pl.CostEstimate(flops=3_000_000_000, bytes_accessed=6_000_000, transcendentals=0),
        name="difference_sums",
    )(*[pltpu.with_memory_space_constraint(operand, pltpu.HBM) for operand in operands])
    return result.reshape(1, BLK, 2, CW)


def solution(mesh):
    placed = (
        P("region", "dev", None, None, None, None),
        P("region", "dev", None, None),
        P("region", "dev", None, None, None),
        P("region", "dev", None),
    )
    return jax.shard_map(
        per_device,
        mesh=mesh,
        in_specs=placed,
        out_specs=P("region", "dev", None, None),
        check_vma=False,
    )
```

```python
import jax
import jax.numpy as jnp
import ml_dtypes
import numpy as np
from jax import lax
from jax.experimental import pallas as pl
from jax.experimental.pallas import tpu as pltpu
from jax.sharding import PartitionSpec as P

BLK = 128
CW = 128
KSIZE = 21
NPROF = 12
NBASIS = 31
SPREADS = (1.0, 2.0, 4.0)
DEGREES = (4, 3, 2)

RES = 8
NX = 4
EDGE = 16
EXT = BLK + 2 * EDGE
DEPTH = 512
CHUNKS = (16, 48, 48, 16)
NQ = len(CHUNKS)
FIRST = tuple(sum(CHUNKS[:q]) for q in range(NQ))
F32 = jnp.float32
BF16 = jnp.bfloat16
MESH = pl.DeviceIdType.MESH


def basis_list():
    listing = []
    offset = 0
    for degree in DEGREES:
        for vertical in range(degree + 1):
            for across in range(degree + 1 - vertical):
                listing.append((offset + vertical, offset + across))
        offset = offset + degree + 1
    return listing


BASIS = basis_list()


def profiles():
    half_width = (KSIZE - 1) // 2
    taps = np.arange(KSIZE, dtype=np.float64) - half_width
    rows = []
    for spread, degree in zip(SPREADS, DEGREES):
        for exponent in range(degree + 1):
            values = (taps / half_width) ** exponent * np.exp(-taps * taps / (2.0 * spread * spread))
            rows.append(values / np.abs(values).sum())
    return np.stack(rows)


def split_np(matrix):
    high = matrix.astype(np.float32).astype(ml_dtypes.bfloat16)
    low = (matrix - high.astype(np.float64)).astype(np.float32).astype(ml_dtypes.bfloat16)
    return high, low


def constant_matrices():
    half_width = (KSIZE - 1) // 2
    prof = profiles()
    wide = np.zeros((CW, NPROF, CW))
    for target in range(CW):
        for tap in range(KSIZE):
            source = target + tap - half_width
            if 0 <= source < CW:
                wide[source, :, target] = prof[:, tap]
    high, low = split_np(wide.reshape(CW, NPROF // 2, 2 * CW).transpose(1, 0, 2))
    across = np.concatenate([high, high, low], axis=1)
    tall = np.zeros((NPROF, BLK, EXT))
    for target in range(BLK):
        for tap in range(KSIZE):
            tall[:, target, (target + tap - half_width) % EXT] = prof[:, tap]
    high, low = split_np(tall)
    pad = np.zeros((NPROF, BLK, DEPTH - 3 * EXT), ml_dtypes.bfloat16)
    down = np.concatenate([high, low, high, pad], axis=2).reshape(NPROF * BLK, DEPTH)
    sums = prof.sum(axis=1)
    norms = np.zeros((8, CW), np.float32)
    for number, (vertical, horizontal) in enumerate(BASIS):
        norms[:, number] = sums[vertical] * sums[horizontal]
    return across, down, norms


def kernel(
    regions,
    sci_hbm, sky_hbm, coef_hbm, start_hbm, across_hbm, down_hbm, norm_hbm,
    out_ref,
    sci, pack, recv, basis, skyvar, modelled, acc, part,
    sky, edge, across, down, wide, tab, tabs, num, nums, tab_s, num_s, coef_ref, start_ref, norm_ref,
    loc_sem, sky_ss, sky_rs, edge_ss, edge_rs, fwd_ss, fwd_rs,
    tab_ss, tab_rs, num_ss, num_rs, sci_ss, sci_rs, red_ss, red_rs,
):
    region = lax.axis_index("region")
    dev = lax.axis_index("dev")
    x = dev // RES
    r = dev % RES
    y = r // 2
    z = r % 2
    total_devs = regions * RES * NX
    whole = region * (RES * NX) + dev

    def order(i):
        return (lax.shift_right_logical(jnp.int32(15394568), jnp.int32(3 * i)) % RES)

    def peer(t):
        return ((y + t // 2) % 4) * 2 + (z + t % 2) % 2

    def giver(t):
        return ((y + 4 - t // 2) % 4) * 2 + (z + t % 2) % 2

    def plane_id(res):
        return {"dev": x * RES + res}

    def line_id(dx):
        return {"dev": ((x + dx) % NX) * RES + r}

    def sky_id(step):
        other = (whole + step + total_devs) % total_devs
        return {"region": other // (RES * NX), "dev": other % (RES * NX)}

    def sci_copy(h, t, slot):
        return pltpu.make_async_remote_copy(
            src_ref=pack[h].at[t], dst_ref=recv[h].at[slot],
            send_sem=sci_ss.at[h, t], recv_sem=sci_rs.at[h, slot],
            device_id=plane_id(peer(t)), device_id_type=MESH)

    def tab_copy(t, slot):
        return pltpu.make_async_remote_copy(
            src_ref=tab, dst_ref=tabs.at[slot],
            send_sem=tab_ss.at[t], recv_sem=tab_rs.at[slot],
            device_id=plane_id(peer(t)), device_id_type=MESH)

    def num_copy(t, slot):
        return pltpu.make_async_remote_copy(
            src_ref=num, dst_ref=nums.at[slot],
            send_sem=num_ss.at[t], recv_sem=num_rs.at[slot],
            device_id=plane_id(peer(t)), device_id_type=MESH)

    def sky_copy(dx, slot):
        return pltpu.make_async_remote_copy(
            src_ref=sky.at[x], dst_ref=sky.at[slot],
            send_sem=sky_ss.at[dx], recv_sem=sky_rs.at[slot],
            device_id=line_id(dx), device_id_type=MESH)

    def fwd_copy(dx, slot):
        return pltpu.make_async_remote_copy(
            src_ref=edge.at[x], dst_ref=edge.at[slot],
            send_sem=fwd_ss.at[dx], recv_sem=fwd_rs.at[slot],
            device_id=line_id(dx), device_id_type=MESH)

    def edge_copy(side):
        rows = pl.ds(2 * (BLK - EDGE), 2 * EDGE) if side == 0 else pl.ds(0, 2 * EDGE)
        return pltpu.make_async_remote_copy(
            src_ref=sky.at[x, rows], dst_ref=edge.at[x_of(side), side],
            send_sem=edge_ss.at[side], recv_sem=edge_rs.at[side],
            device_id=sky_id(1 if side == 0 else -1), device_id_type=MESH)

    def x_of(side):
        other = (whole + (1 if side == 0 else -1) + total_devs) % total_devs
        return (other % (RES * NX)) // RES

    def edge_arrival(side):
        rows = pl.ds(2 * (BLK - EDGE), 2 * EDGE) if side == 0 else pl.ds(0, 2 * EDGE)
        return pltpu.make_async_remote_copy(
            src_ref=sky.at[x, rows], dst_ref=edge.at[x, side],
            send_sem=edge_ss.at[side], recv_sem=edge_rs.at[side],
            device_id=sky_id(1 if side == 0 else -1), device_id_type=MESH)

    def red_copy(h, dx, slot):
        return pltpu.make_async_remote_copy(
            src_ref=acc[h].at[(x + dx) % NX], dst_ref=part[h].at[slot],
            send_sem=red_ss.at[h, dx], recv_sem=red_rs.at[h, slot],
            device_id=line_id(dx), device_id_type=MESH)

    def load(source, target, number):
        copy = pltpu.make_async_copy(source, target, loc_sem.at[number])
        copy.start()
        return copy

    def load_science(q):
        rows = pl.ds(2 * FIRST[q], 2 * CHUNKS[q])
        return load(sci_hbm.at[:, :, rows], sci[q], 9 + q)

    start_load = load(start_hbm, start_ref, 6)
    sky_load = load(sky_hbm, sky.at[x], 0)
    coef_load = load(coef_hbm, coef_ref, 7)
    norm_load = load(norm_hbm, norm_ref, 8)
    sci_load = [load_science(0)]

    barrier = pltpu.get_barrier_semaphore()

    def greet(t, carry):
        pl.semaphore_signal(barrier, inc=1, device_id=plane_id(peer(t)), device_id_type=MESH)
        return carry

    lax.fori_loop(1, RES, greet, 0)
    for dx in range(1, NX):
        pl.semaphore_signal(barrier, inc=1, device_id=line_id(dx), device_id_type=MESH)

    has_next = whole < total_devs - 1
    has_previous = whole > 0
    for step, there in ((1, has_next), (-1, has_previous)):
        @pl.when(there)
        def _():
            pl.semaphore_signal(barrier, inc=1, device_id=sky_id(step), device_id_type=MESH)

    sci_load += [load_science(q) for q in range(1, NQ)]
    across_load = load(across_hbm, across, 2)
    down_load = load(down_hbm, down, 3)

    lanes = lax.broadcasted_iota(jnp.int32, (8, CW), 1)
    start_load.wait()
    starts = (start_ref[0, 0], start_ref[0, 1])
    num[...] = jnp.where(lanes[0:1] == 0, starts[0], starts[1])
    sky_load.wait()
    ends = (whole + total_devs - 1) // total_devs + (2 * total_devs - 2 - whole) // total_devs
    pl.semaphore_wait(barrier, RES - 1 + NX - 1 + ends)

    for side, there in ((0, has_next), (1, has_previous)):
        @pl.when(there)
        def _():
            edge_copy(side).start()
    for dx in range(1, NX):
        sky_copy(dx, x).start()

    def chosen(q, res, e):
        block = lax.rem(res - starts[e] + 4 * RES, RES)
        return sci[q][e, block]

    for q in range(NQ):
        sci_load[q].wait()

        def give(i, carry):
            t = order(i)
            for e in range(2):
                pack[q][t, e] = chosen(q, peer(t), e)
            sci_copy(q, t, r).start()
            return carry

        lax.fori_loop(1, RES, give, 0)
        for e in range(2):
            recv[q][r, e] = chosen(q, r, e)
        if q == 0:
            coef_load.wait()
            norm_load.wait()
            tab[...] = jnp.zeros((8, CW), F32)
            for term in range(3):
                tab[2 * term : 2 * term + 2, 0:NBASIS] = coef_ref[term]
            raw = tab[...]
            weighted = jnp.sum(raw * norm_ref[...], axis=1, keepdims=True)
            tab[...] = jnp.where(lanes == NBASIS, weighted, raw)
            tabs[r] = tab[...]
            nums[r] = num[...]

            def give_tables(i, carry):
                t = order(i)
                tab_copy(t, r).start()
                num_copy(t, r).start()
                return carry

            lax.fori_loop(1, RES, give_tables, 0)
        if q == 2:
            for side, there in ((0, has_previous), (1, has_next)):
                @pl.when(there)
                def _():
                    edge_arrival(side).wait_recv()

                @pl.when(jnp.logical_not(there))
                def _():
                    edge[x, side] = jnp.zeros((2 * EDGE, CW), F32)
            for dx in range(1, NX):
                fwd_copy(dx, x).start()

    for q in range(NQ):
        acc[q][...] = jnp.zeros(acc[q].shape, F32)
    for block in range(NX):
        for profile in range(NPROF):
            wide[block, profile, 3 * EXT : DEPTH, :] = jnp.zeros((DEPTH - 3 * EXT, CW), BF16)
    across_load.wait()

    def spread_across(rows, places):
        high = rows.astype(BF16)
        rest = (rows - high.astype(F32)).astype(BF16)
        lhs = jnp.concatenate([high, rest, high], axis=1)
        for tile in range(NPROF // 2):
            both = jnp.dot(lhs, across[tile], preferred_element_type=F32)
            for side in range(2):
                values = both[:, side * CW : (side + 1) * CW]
                high = values.astype(BF16)
                rest = (values - high.astype(F32)).astype(BF16)
                profile = 2 * tile + side
                for block, first, count, to in places:
                    wide[block, profile, to : to + count, :] = high[first : first + count]
                    wide[block, profile, EXT + to : EXT + to + count, :] = high[first : first + count]
                    wide[block, profile, 2 * EXT + to : 2 * EXT + to + count, :] = rest[first : first + count]

    def body_rows(block):
        for q in range(NQ):
            skyvar[q][block] = sky[block, pl.ds(2 * FIRST[q] + 1, CHUNKS[q], stride=2), :]
        return sky[block, pl.ds(0, BLK, stride=2), :]

    def smooth(pair):
        for across_profile in range(NPROF):
            users = [(k, v) for k, (v, a) in enumerate(BASIS) if a == across_profile]
            low_v = users[0][1]
            result = jnp.dot(
                down[low_v * BLK : (low_v + len(users)) * BLK, :],
                jnp.concatenate([wide[2 * pair, across_profile], wide[2 * pair + 1, across_profile]], axis=1),
                preferred_element_type=F32)
            for place, (k, v) in enumerate(users):
                for side in range(2):
                    for q in range(NQ):
                        row = place * BLK + FIRST[q]
                        basis[q][2 * pair + side, k] = result[row : row + CHUNKS[q], side * CW : (side + 1) * CW]

    near = 2 * (x // 2) + 1 - x % 2
    far = 2 * (1 - x // 2)
    spread_across(body_rows(x), [(x, 0, BLK, 0)])
    sky_copy(1, near).wait_recv()
    spread_across(body_rows(near), [(near, 0, BLK, 0)])

    fwd_copy(1, near).wait_recv()
    for side in range(2):
        fwd_copy(1, far + side).wait_recv()
    rims = []
    for block in range(NX):
        top = edge[block, 0, pl.ds(0, EDGE, stride=2), :]
        low = edge[block, 1, pl.ds(0, EDGE, stride=2), :]
        rims += [low, top]
    spread_across(
        jnp.concatenate(rims, axis=0), [(block, 2 * EDGE * block, 2 * EDGE, BLK) for block in range(NX)])
    down_load.wait()
    smooth(x // 2)
    for side in range(2):
        sky_copy(1, far + side).wait_recv()
    spread_across(
        jnp.concatenate([body_rows(far), body_rows(far + 1)], axis=0),
        [(far, 0, BLK, 0), (far + 1, BLK, BLK, 0)])
    smooth(1 - x // 2)

    def tables(t, carry):
        tab_copy(t, giver(t)).wait_recv()
        num_copy(t, giver(t)).wait_recv()
        return carry

    lax.fori_loop(1, RES, tables, 0)
    tab_move = pltpu.make_async_copy(tabs, tab_s, loc_sem.at[4])
    tab_move.start()
    num_move = pltpu.make_async_copy(nums, num_s, loc_sem.at[5])
    num_move.start()
    tab_move.wait()
    num_move.wait()

    xs = (2.0 * lanes.astype(F32) + 1.0) / CW - 1.0

    def model(q, t):
        source = giver(t)
        shape = (CHUNKS[q] // 8, 8, CW)
        rows = (8 * lax.broadcasted_iota(jnp.int32, shape, 0) + lax.broadcasted_iota(jnp.int32, shape, 1)).astype(F32)
        ys_base = (2.0 * rows + 1.0) / (RES * BLK)
        for e in range(2):
            start = num_s[source, 0, e]
            place = lax.rem(r - start + 4 * RES, RES)
            block = (start + place) // RES
            flat = jnp.zeros(shape, F32)
            slope = jnp.zeros(shape, F32)
            for k in range(NBASIS):
                image = basis[q][block, k].reshape(shape)
                factor = tab_s[source, e, k] + tab_s[source, 2 + e, k] * xs
                flat = flat + factor[None] * image
                slope = slope + tab_s[source, 4 + e, k] * image
            y0 = (place * BLK + FIRST[q]).astype(F32)
            ys = ys_base + (y0 * (2.0 / (RES * BLK)) - 1.0)
            gain = (tab_s[source, e, NBASIS] + tab_s[source, 2 + e, NBASIS] * xs)[None] + tab_s[
                source, 4 + e, NBASIS] * ys
            behind = skyvar[q][block].reshape(shape)
            modelled[q][source, e, 0] = (flat + ys * slope).reshape(CHUNKS[q], CW)
            modelled[q][source, e, 1] = (gain * gain * behind).reshape(CHUNKS[q], CW)

    def add(q, t):
        source = giver(t)
        count = CHUNKS[q]
        found = []
        for e in range(2):
            start = num_s[source, 0, e]
            block = (start + lax.rem(r - start + 4 * RES, RES)) // RES
            flux = recv[q][source, e, pl.ds(0, count, stride=2), :]
            noise = recv[q][source, e, pl.ds(1, count, stride=2), :]
            weight = 1.0 / (noise + modelled[q][source, e, 1])
            found.append((block, (flux - modelled[q][source, e, 0]) * weight, weight))
        for target in range(NX):
            for plane in range(2):
                span = slice(plane * count, (plane + 1) * count)
                old = acc[q][target, span, :]
                for block, diff, weight in found:
                    old = old + jnp.where(block == target, weight if plane else diff, 0.0)
                acc[q][target, span, :] = old

    def finish(q):
        for dx in range(1, NX):
            red_copy(q, dx, (x + dx) % NX).wait_recv()
        count = CHUNKS[q]
        total = acc[q][x]
        for dx in range(1, NX):
            total = total + part[q][(x + dx) % NX]
        for plane in range(2):
            out_ref[pl.ds(2 * FIRST[q] + plane, count, stride=2), :] = total[plane * count : (plane + 1) * count]

    for q in range(NQ):
        def prepare(t, carry):
            model(q, t)
            return carry

        lax.fori_loop(0, RES, prepare, 0)
        add(q, 0)

        def take(i, carry):
            t = order(i)
            sci_copy(q, t, giver(t)).wait_recv()
            add(q, t)
            return carry

        lax.fori_loop(1, RES, take, 0)
        for dx in range(1, NX):
            red_copy(q, dx, x).start()
        if q > 0:
            finish(q - 1)
    finish(NQ - 1)

    for side, there in ((0, has_next), (1, has_previous)):
        @pl.when(there)
        def _():
            edge_copy(side).wait_send()
    for dx in range(1, NX):
        sky_copy(dx, x).wait_send()
        fwd_copy(dx, x).wait_send()
        for q in range(NQ):
            red_copy(q, dx, x).wait_send()

    def sent(t, carry):
        tab_copy(t, r).wait_send()
        num_copy(t, r).wait_send()
        for q in range(NQ):
            sci_copy(q, t, r).wait_send()
        return carry

    lax.fori_loop(1, RES, sent, 0)


def per_device(science, coadd, coefficients, strip_start):
    regions = lax.axis_size("region")
    across_np, down_np, norms_np = constant_matrices()
    sci = science.reshape(2, RES, 2 * BLK, CW)
    sky = coadd.reshape(2 * BLK, CW)
    coef = jnp.transpose(coefficients[0, 0], (2, 0, 1))
    starts = strip_start[0]
    dma = pltpu.SemaphoreType.DMA
    def chunked(*lead):
        return [pltpu.VMEM((*lead, 2 * count, CW), F32) for count in CHUNKS]

    def single(*lead):
        return [pltpu.VMEM((*lead, count, CW), F32) for count in CHUNKS]

    scratch = [
        chunked(2, RES), chunked(RES, 2), chunked(RES, 2),
        single(NX, NBASIS), single(NX), single(RES, 2, 2),
        chunked(NX), chunked(NX),
        pltpu.VMEM((NX, 2 * BLK, CW), F32),
        pltpu.VMEM((NX, 2, 2 * EDGE, CW), F32),
        pltpu.VMEM(across_np.shape, BF16),
        pltpu.VMEM(down_np.shape, BF16),
        pltpu.VMEM((NX, NPROF, DEPTH, CW), BF16),
        pltpu.VMEM((8, CW), F32),
        pltpu.VMEM((RES, 8, CW), F32),
        pltpu.VMEM((1, CW), jnp.int32),
        pltpu.VMEM((RES, 1, CW), jnp.int32),
        pltpu.SMEM((RES, 8, CW), F32),
        pltpu.SMEM((RES, 1, CW), jnp.int32),
        pltpu.VMEM((3, 2, NBASIS), F32),
        pltpu.SMEM((1, 2), jnp.int32),
        pltpu.VMEM((8, CW), F32),
        dma((9 + NQ,)),
        dma((NX,)), dma((NX,)),
        dma((2,)), dma((2,)),
        dma((NX,)), dma((NX,)),
        dma((RES,)), dma((RES,)),
        dma((RES,)), dma((RES,)),
        dma((NQ, RES)), dma((NQ, RES)),
        dma((NQ, NX)), dma((NQ, NX)),
    ]
    operands = (sci, sky, coef, starts, jnp.asarray(across_np), jnp.asarray(down_np), jnp.asarray(norms_np))
    hbm = pl.BlockSpec(memory_space=pl.ANY)
    vmem = pl.BlockSpec(memory_space=pltpu.VMEM)
    result = pl.pallas_call(
        lambda *refs: kernel(regions, *refs),
        out_shape=jax.ShapeDtypeStruct((2 * BLK, CW), F32),
        in_specs=[hbm] * 7,
        out_specs=vmem,
        scratch_shapes=scratch,
        compiler_params=pltpu.CompilerParams(
            collective_id=0, has_side_effects=True, vmem_limit_bytes=52 * 1024 * 1024),
        cost_estimate=pl.CostEstimate(flops=3_000_000_000, bytes_accessed=6_000_000, transcendentals=0),
        name="difference_sums",
    )(*[pltpu.with_memory_space_constraint(operand, pltpu.HBM) for operand in operands])
    return result.reshape(1, BLK, 2, CW)


def solution(mesh):
    placed = (
        P("region", "dev", None, None, None, None),
        P("region", "dev", None, None),
        P("region", "dev", None, None, None),
        P("region", "dev", None),
    )
    return jax.shard_map(
        per_device,
        mesh=mesh,
        in_specs=placed,
        out_specs=P("region", "dev", None, None),
        check_vma=False,
    )
```
